128 devices in a mesh: prod: 4 (over y_lo, core), sae: 32 (over x, z, y_hi).
Axes of the slice: x: 4, y: 4 (y_hi: 2, y_lo: 2; y = y_hi * 2 + y_lo), z: 4, core: 2. Of those that a mesh axis runs over, the one named last changes fastest.
Arguments:
- head_outputs: bfloat16 [512, 2048], P('sae', 'prod'), may hold values from -13 to 13
- out_weight: bfloat16 [2048, 4608], P('prod'), may hold values from -0.28726213 to 0.28726213
- residual_input: bfloat16 [512, 4608], P('sae'), may hold values from -6 to 6
- post_gain: float32 [4608], replicated, may hold values from 0.1 to 1.9
- encoder_weight: bfloat16 [4608, 65536], P(None, ('prod', 'sae')), may hold values from -0.09375 to 0.09375
- encoder_bias: float32 [65536], P(('prod', 'sae')), may hold values from -3 to 3
- decoder_weight: bfloat16 [65536, 4608], P(('prod', 'sae')), may hold values from -0.15625 to 0.15625
- decoder_bias: float32 [4608], replicated, may hold values from -3 to 3
Outputs:
- grad_encoder: bfloat16 [4608, 65536], P(None, ('prod', 'sae'))
- grad_encoder_bias: float32 [65536], P(('prod', 'sae'))
- grad_decoder: bfloat16 [65536, 4608], P(('prod', 'sae'))
The draws below stay inside these ranges and needn't reach their ends.
All inputs are finite; a program needn't handle non-finite values.
Results may differ from the reference program's by a relative error of at most 0.0064.
Values may be sent and summed in bfloat16 or wider, within the bound.
No kernel may reach another device: no remote copies, remote signals or barrier semaphores. Data moves between devices by JAX's collectives and lax.ppermute only.
A program may use at most 128 MiB of HBM per device.

```python
import jax
import jax.numpy as jnp
from jax import lax

D = 4608
HD = 128
HEADS = 16
LAT_DEV = 512
TOKENS = 512
LATENTS = 65536


def apply_scales(key, base, row_ratio, col_ratio, fan_in):
    key_row, key_col = jax.random.split(key)
    row_half = 0.5 * jnp.log(row_ratio)
    col_half = 0.5 * jnp.log(col_ratio)
    row_scale = jnp.exp(jax.random.uniform(key_row, (base.shape[0], 1), jnp.float32, -row_half, row_half))
    col_scale = jnp.exp(jax.random.uniform(key_col, (1, base.shape[1]), jnp.float32, -col_half, col_half))
    return base * row_scale * col_scale / jnp.sqrt(jnp.float32(fan_in))


def draw_head_outputs(key, part):
    key = jax.random.fold_in(key, 11)
    key_base, key_rest = jax.random.split(key)
    shape = (TOKENS, HEADS * HD)
    base = jnp.clip(jax.random.normal(key_base, shape, jnp.float32), -4.0, 4.0)
    spread = 10.0
    return apply_scales(key_rest, base, spread, 1.0, 1.0).astype(jnp.bfloat16)


def draw_out_weight(key, part):
    key = jax.random.fold_in(key, 23)
    key_base, key_rest = jax.random.split(key)
    shape = (HEADS * HD, D)
    base = jnp.clip(jax.random.normal(key_base, shape, jnp.float32), -4.0, 4.0)
    spread = 10.0
    return apply_scales(key_rest, base, 1.0, spread, HEADS * HD).astype(jnp.bfloat16)


def draw_decoder_weight(key, part):
    key = jax.random.fold_in(key, 37)
    key_base, key_rest = jax.random.split(key)
    shape = (LATENTS, D)
    base = jnp.clip(jax.random.normal(key_base, shape, jnp.float32), -4.0, 4.0)
    spread = 10.0
    return apply_scales(key_rest, base, spread, spread, LATENTS).astype(jnp.bfloat16)


def level_of(stream_key, extent, cuts, least, high):
    def one(dim, blocks):
        heights = jax.random.uniform(jax.random.fold_in(jax.random.fold_in(stream_key, 6), dim), (blocks,), jnp.float32, least / len(cuts), high / len(cuts))
        return jnp.repeat(jnp.exp(heights), extent[dim] // blocks).reshape((-1,) + (1,) * (len(extent) - dim - 1))

    level = one(*cuts[0])
    for cut in cuts[1:]:
        level = level * one(*cut)
    return level


def normal_values(key, dims, scale, most, cuts=(), dtype=jnp.bfloat16):
    factor_of = level_of(key, dims, cuts, -0.22, 0.18) if cuts else 1.0
    array = jax.random.normal(key, dims, jnp.float32) * scale * factor_of
    return jnp.minimum(jnp.maximum(array, -most), most).astype(dtype)


def setup_inputs(seed: int = 0) -> dict:
    arg_keys = jax.random.split(jax.random.key(seed), 9)
    head_outputs = draw_head_outputs(jax.random.fold_in(arg_keys[8], 71), 0)
    out_weight = draw_out_weight(jax.random.fold_in(arg_keys[8], 71), 0)
    residual_input = normal_values(arg_keys[2], (TOKENS, D), 1.0, 6.0, ((0, 32),))
    post_gain = jnp.clip(1.0 + 0.18 * jax.random.normal(arg_keys[3], (D,), jnp.float32), 0.1, 1.9)
    encoder_weight = normal_values(arg_keys[4], (D, LATENTS), D ** -0.5, 0.09375, ((1, 128),))
    encoder_bias = normal_values(arg_keys[5], (LATENTS,), 0.5, 3.0, ((0, 128),), jnp.float32)
    decoder_weight = draw_decoder_weight(jax.random.fold_in(arg_keys[8], 71), 0)
    decoder_bias = normal_values(arg_keys[7], (D,), 0.5, 3.0, (), jnp.float32)
    return dict(head_outputs=head_outputs, out_weight=out_weight, residual_input=residual_input, post_gain=post_gain, encoder_weight=encoder_weight, encoder_bias=encoder_bias, decoder_weight=decoder_weight, decoder_bias=decoder_bias)


sparsity_weight = 4.0
norm_epsilon = 1e-06

def reference(head_outputs, out_weight, residual_input, post_gain, encoder_weight, encoder_bias, decoder_weight, decoder_bias):
    projected = jnp.dot(head_outputs, out_weight, preferred_element_type=jnp.float32)
    normed = projected * lax.rsqrt(lax.optimization_barrier(jnp.mean(projected * projected, axis=1, keepdims=True)) + norm_epsilon) * post_gain
    stream = (residual_input.astype(jnp.float32) + normed).astype(jnp.bfloat16)
    centred = (stream.astype(jnp.float32) - decoder_bias).astype(jnp.bfloat16)
    block_count = LATENTS // LAT_DEV
    encoder_blocks = jnp.transpose(encoder_weight.reshape(D, block_count, LAT_DEV), (1, 0, 2))
    bias_blocks = encoder_bias.reshape(block_count, LAT_DEV)
    decoder_blocks = decoder_weight.reshape(block_count, LAT_DEV, D)

    def activate(encoder_part, bias_part):
        preact = jnp.dot(centred, encoder_part, preferred_element_type=jnp.float32) + bias_part
        rectified = jnp.maximum(preact, 0.0)
        return (rectified, jnp.square(rectified).astype(jnp.bfloat16))

    def forward(running, pieces):
        rectified, activations = activate(pieces[0], pieces[1])
        return (running + jnp.dot(activations, pieces[2], preferred_element_type=jnp.float32), None)
    summed, unused = lax.scan(forward, jnp.zeros((TOKENS, D), jnp.float32), (encoder_blocks, bias_blocks, decoder_blocks))
    grad_recon = (2.0 * (summed + decoder_bias - stream.astype(jnp.float32)) / TOKENS).astype(jnp.bfloat16)

    def backward(pieces):
        rectified, activations = activate(pieces[0], pieces[1])
        decoder_part = pieces[2]
        decoder_wide = decoder_part.astype(jnp.float32)
        row_norms = jnp.sqrt(lax.optimization_barrier(jnp.sum(decoder_wide * decoder_wide, axis=1)) + norm_epsilon)
        grad_acts = jnp.dot(grad_recon, decoder_part.T, preferred_element_type=jnp.float32) + sparsity_weight * row_norms / TOKENS
        grad_pre = (grad_acts * 2.0 * rectified).astype(jnp.bfloat16)
        encoder_grad = jnp.dot(centred.T, grad_pre, preferred_element_type=jnp.float32).astype(jnp.bfloat16)
        bias_grad = lax.optimization_barrier(jnp.sum(grad_pre.astype(jnp.float32), axis=0))
        act_sum = lax.optimization_barrier(jnp.sum(activations.astype(jnp.float32), axis=0))
        decoder_grad = jnp.dot(activations.T, grad_recon, preferred_element_type=jnp.float32)
        decoder_grad = decoder_grad + sparsity_weight / TOKENS * (act_sum / row_norms)[:, None] * decoder_wide
        return (encoder_grad, bias_grad, decoder_grad.astype(jnp.bfloat16))
    results = lax.map(backward, (encoder_blocks, bias_blocks, decoder_blocks))
    grad_encoder = jnp.transpose(results[0], (1, 0, 2)).reshape(D, LATENTS)
    return (grad_encoder, results[1].reshape(LATENTS), results[2].reshape(LATENTS, D))
```

```python
import jax
import jax.numpy as jnp
from jax import lax
from jax.sharding import PartitionSpec as P

sparsity_weight = 4.0
norm_epsilon = 1e-06
TOKENS = 512
D = 4608
HALF = D // 2
AXES = ("prod", "sae")
bf16 = jnp.bfloat16
f32 = jnp.float32


def place(x, y, z, c):
    return ((y % 2) * 2 + c) * 32 + (x * 4 + z) * 2 + y // 2


def route(step):
    pairs = []
    for x in range(4):
        for y in range(4):
            for z in range(4):
                for c in range(2):
                    tx, ty, tz, tc = step(x, y, z, c)
                    pairs.append((place(x, y, z, c), place(tx % 4, ty % 4, tz % 4, tc % 2)))
    return pairs


def move(value, step):
    return lax.ppermute(value, AXES, route(step))


def to_core(value):
    return move(value, lambda x, y, z, c: (x, y, z, 1 - c))


def to_major(value, d):
    return move(value, lambda x, y, z, c: (x + d, y, z, c) if c == 0 else (x, y, z + d, c))


def to_minor(value, d):
    return move(value, lambda x, y, z, c: (x, y, z + d, c) if c == 0 else (x + d, y, z, c))


def to_y(value, d):
    return move(value, lambda x, y, z, c: (x, y + d, z, c))


def gather(value, to):
    return [value] + [to(value, -d) for d in (1, 2, 3)]


def scatter_sum(pieces, to):
    got = [to(pieces[d], d) for d in (1, 2, 3)]
    total = pieces[0].astype(f32)
    for g in got:
        total = total + g.astype(f32)
    return total


def swap_blocks(value):
    return value.reshape(4, 4, 32, value.shape[-1]).transpose(1, 0, 2, 3).reshape(value.shape)


def local(
    head_outputs,
    out_weight,
    residual_input,
    post_gain,
    encoder_weight,
    encoder_bias,
    decoder_weight,
    decoder_bias,
):
    here = lax.axis_index("prod")
    low = here // 2 == 0
    first = here % 2 == 0

    def own_half(v):
        return jnp.where(first, v[..., :HALF], v[..., HALF:])

    def other_half(v):
        return jnp.where(first, v[..., HALF:], v[..., :HALF])

    heads = jnp.where(low, head_outputs, jnp.roll(head_outputs, 8, axis=0))
    partial_value = jnp.dot(heads, out_weight, preferred_element_type=f32)
    both = own_half(partial_value) + to_core(other_half(partial_value))
    partner = lax.ppermute(both[8:], "prod", [(0, 2), (2, 0), (1, 3), (3, 1)])
    projected = both[:8] + partner
    squares = jnp.broadcast_to(jnp.sum(projected * projected, axis=1, keepdims=True), (8, 128))
    squares = (squares + to_core(squares))[:, :1]
    gain = own_half(post_gain)
    normed = projected * lax.rsqrt(squares / D + norm_epsilon) * gain
    residual = own_half(jnp.where(low, residual_input[:8], residual_input[8:]))
    stream = (residual.astype(f32) + normed).astype(bf16)

    bias_own = own_half(decoder_bias)
    stream = jnp.concatenate(gather(stream, to_y))
    centred = (stream.astype(f32) - bias_own).astype(bf16)
    centred = jnp.concatenate(gather(centred, to_minor))
    centred_own = jnp.concatenate(gather(centred, to_major))
    centred_other = swap_blocks(to_core(centred_own))

    def whole(own, other):
        return jnp.concatenate(
            [jnp.where(first, own, other), jnp.where(first, other, own)], axis=1
        )

    centred = whole(centred_own, centred_other)
    preact = jnp.dot(centred, encoder_weight, preferred_element_type=f32) + encoder_bias
    rectified = jnp.maximum(preact, 0.0)
    activations = jnp.square(rectified).astype(bf16)

    recon = jnp.dot(activations, decoder_weight, preferred_element_type=f32).astype(bf16)
    recon = own_half(recon).astype(f32) + to_core(swap_blocks(other_half(recon))).astype(f32)
    recon = recon.astype(bf16)
    recon = scatter_sum(jnp.split(recon, 4), to_major).astype(bf16)
    recon = scatter_sum(jnp.split(recon, 4), to_minor).astype(bf16)
    summed = recon.astype(f32)
    for d in (1, 2, 3):
        summed = summed + jnp.roll(to_y(recon, -d), 8 * d, axis=0).astype(f32)
    grad_recon = (2.0 * (summed + bias_own - stream.astype(f32)) / TOKENS).astype(bf16)

    errors = jnp.concatenate(gather(grad_recon, to_minor))
    errors_own = jnp.concatenate(gather(errors, to_major))
    all_errors = whole(errors_own, swap_blocks(to_core(errors_own)))

    decoder_wide = decoder_weight.astype(f32)
    row_norms = jnp.sqrt(jnp.sum(decoder_wide * decoder_wide, axis=1) + norm_epsilon)
    grad_acts = jnp.einsum("td,ld->tl", all_errors, decoder_weight, preferred_element_type=f32)
    grad_acts = grad_acts + sparsity_weight * row_norms / TOKENS
    grad_pre = (grad_acts * 2.0 * rectified).astype(bf16)
    grad_encoder = jnp.einsum("td,tl->dl", centred, grad_pre, preferred_element_type=f32)
    grad_encoder_bias = jnp.sum(grad_pre.astype(f32), axis=0)
    act_sum = jnp.sum(activations.astype(f32), axis=0)
    grad_decoder = jnp.einsum("tl,td->ld", activations, all_errors, preferred_element_type=f32)
    grad_decoder = (
        grad_decoder + sparsity_weight / TOKENS * (act_sum / row_norms)[:, None] * decoder_wide
    )
    return (grad_encoder.astype(bf16), grad_encoder_bias, grad_decoder.astype(bf16))


def solution(mesh):
    placed = (
        P("sae", "prod"),
        P("prod", None),
        P("sae", None),
        P(),
        P(None, ("prod", "sae")),
        P(("prod", "sae")),
        P(("prod", "sae"), None),
        P(),
    )
    return jax.shard_map(
        local,
        mesh=mesh,
        in_specs=placed,
        out_specs=(P(None, ("prod", "sae")), P(("prod", "sae")), P(("prod", "sae"), None)),
        check_vma=False,
    )
```

```python
import jax
import jax.numpy as jnp
from jax import lax
from jax.sharding import PartitionSpec as P

sparsity_weight = 4.0
norm_epsilon = 1e-06
TOKENS = 512
D = 4608
HALF = D // 2
AXES = ("prod", "sae")
bf16 = jnp.bfloat16
f32 = jnp.float32


def place(x, y, z, c):
    return ((y % 2) * 2 + c) * 32 + (x * 4 + z) * 2 + y // 2


def route(step):
    pairs = []
    for x in range(4):
        for y in range(4):
            for z in range(4):
                for c in range(2):
                    tx, ty, tz, tc = step(x, y, z, c)
                    pairs.append((place(x, y, z, c), place(tx % 4, ty % 4, tz % 4, tc % 2)))
    return pairs


def move(value, step):
    return lax.ppermute(value, AXES, route(step))


def to_core(value):
    return move(value, lambda x, y, z, c: (x, y, z, 1 - c))


def to_major(value, d):
    return move(value, lambda x, y, z, c: (x + d, y, z, c) if c == 0 else (x, y, z + d, c))


def team(members):
    found = {}
    for x in range(4):
        for y in range(4):
            for z in range(4):
                for c in range(2):
                    group, rank = members(x, y, z, c)
                    found.setdefault(group, []).append((rank, place(x, y, z, c)))
    return [[device for _, device in sorted(found[g])] for g in sorted(found)]


def axis_pair(x, z, c):
    return (x, z) if c == 0 else (z, x)


def team8(x, y, z, c):
    major, minor = axis_pair(x, z, c)
    return (c, major, y % 2), (minor, y // 2)


def team16(x, y, z, c):
    major, minor = axis_pair(x, z, c)
    return (c, major), (minor, y)


def exchange(value, members):
    return lax.all_to_all(
        value, AXES, 0, 0, axis_index_groups=team(members), tiled=True
    )


def gather(value, to):
    return [value] + [to(value, -d) for d in (1, 2, 3)]


def swap_blocks(value):
    return value.reshape(4, 4, 32, value.shape[-1]).transpose(1, 0, 2, 3).reshape(value.shape)


def turn(value, by):
    blocks = value.reshape(4, 32, value.shape[-1])
    blocks = lax.dynamic_slice_in_dim(jnp.concatenate([blocks, blocks]), by, 4)
    return blocks.reshape(value.shape)


def local(
    head_outputs,
    out_weight,
    residual_input,
    post_gain,
    encoder_weight,
    encoder_bias,
    decoder_weight,
    decoder_bias,
):
    here = lax.axis_index("prod")
    there = lax.axis_index("sae")
    low = here // 2 == 0
    core = here % 2
    first = core == 0
    minor = jnp.where(first, there // 2 % 4, there // 8)

    def own_half(v):
        return jnp.where(first, v[..., :HALF], v[..., HALF:])

    def other_half(v):
        return jnp.where(first, v[..., HALF:], v[..., :HALF])

    encoder_own = lax.dynamic_slice_in_dim(encoder_weight, core * HALF, HALF, 0)
    encoder_other = lax.dynamic_slice_in_dim(encoder_weight, (1 - core) * HALF, HALF, 0)
    decoder_own = own_half(decoder_weight)
    decoder_other = other_half(decoder_weight)

    partial_value = jnp.dot(head_outputs, out_weight, preferred_element_type=f32)
    both = own_half(partial_value) + to_core(other_half(partial_value))
    projected = both + lax.ppermute(both, "prod", [(0, 2), (2, 0), (1, 3), (3, 1)])
    squares = jnp.broadcast_to(jnp.sum(projected * projected, axis=1, keepdims=True), (16, 128))
    squares = (squares + to_core(squares))[:, :1]
    gain = own_half(post_gain)
    normed = projected * lax.rsqrt(squares / D + norm_epsilon) * gain
    stream = (own_half(residual_input).astype(f32) + normed).astype(bf16)

    bias_own = own_half(decoder_bias)
    centred = (stream.astype(f32) - bias_own).astype(bf16)
    centred = exchange(jnp.broadcast_to(centred, (8, 16, HALF)), team8)
    centred = turn(centred.reshape(128, HALF), minor)
    centred_own = gather(centred, to_major)
    centred_other = jnp.concatenate([to_core(piece) for piece in centred_own])
    centred_own = jnp.concatenate(centred_own)

    def whole(own, other):
        other = swap_blocks(other)
        return jnp.concatenate(
            [jnp.where(first, own, other), jnp.where(first, other, own)], axis=1
        )

    preact = jnp.dot(centred_own, encoder_own, preferred_element_type=f32)
    preact = preact + swap_blocks(
        jnp.dot(centred_other, encoder_other, preferred_element_type=f32)
    )
    rectified = jnp.maximum(preact + encoder_bias, 0.0)
    activations = jnp.square(rectified).astype(bf16)
    swapped = swap_blocks(activations)

    pieces = []
    for d in range(4):
        rows = slice(128 * d, 128 * d + 128)
        got = jnp.dot(swapped[rows], decoder_other, preferred_element_type=f32).astype(bf16)
        mine = jnp.dot(activations[rows], decoder_own, preferred_element_type=f32)
        piece = (mine + to_core(got).astype(f32)).astype(bf16)
        pieces.append(to_major(piece, d) if d else piece)
    recon = sum(piece.astype(f32) for piece in pieces).astype(bf16)
    recon = exchange(turn(recon, (4 - minor) % 4).reshape(16, 8, HALF), team16)
    summed = jnp.sum(recon.astype(f32), axis=0)
    own_stream = jnp.where(low, stream[:8], stream[8:])
    grad_recon = (2.0 * (summed + bias_own - own_stream.astype(f32)) / TOKENS).astype(bf16)

    errors = exchange(jnp.broadcast_to(grad_recon, (16, 8, HALF)), team16)
    errors = turn(errors.reshape(128, HALF), minor)
    errors_own = gather(errors, to_major)
    errors_other = jnp.concatenate([to_core(piece) for piece in errors_own])
    errors_own = jnp.concatenate(errors_own)
    all_errors = whole(errors_own, errors_other)
    centred = whole(centred_own, centred_other)

    decoder_wide = decoder_weight.astype(f32)
    row_norms = jnp.sqrt(jnp.sum(decoder_wide * decoder_wide, axis=1) + norm_epsilon)
    grad_acts = jnp.einsum("td,ld->tl", errors_own, decoder_own, preferred_element_type=f32)
    grad_acts = grad_acts + swap_blocks(
        jnp.einsum("td,ld->tl", errors_other, decoder_other, preferred_element_type=f32)
    )
    grad_acts = grad_acts + sparsity_weight * row_norms / TOKENS
    grad_pre = (grad_acts * 2.0 * rectified).astype(bf16)
    grad_encoder = jnp.einsum("td,tl->dl", centred, grad_pre, preferred_element_type=f32)
    grad_encoder_bias = jnp.sum(grad_pre.astype(f32), axis=0)
    act_sum = jnp.sum(activations.astype(f32), axis=0)
    grad_decoder = jnp.einsum("tl,td->ld", activations, all_errors, preferred_element_type=f32)
    grad_decoder = (
        grad_decoder + sparsity_weight / TOKENS * (act_sum / row_norms)[:, None] * decoder_wide
    )
    return (grad_encoder.astype(bf16), grad_encoder_bias, grad_decoder.astype(bf16))


def solution(mesh):
    placed = (
        P("sae", "prod"),
        P("prod", None),
        P("sae", None),
        P(),
        P(None, ("prod", "sae")),
        P(("prod", "sae")),
        P(("prod", "sae"), None),
        P(),
    )
    return jax.shard_map(
        local,
        mesh=mesh,
        in_specs=placed,
        out_specs=(P(None, ("prod", "sae")), P(("prod", "sae")), P(("prod", "sae"), None)),
        check_vma=False,
    )
```

```python
import functools

import jax
import jax.numpy as jnp
from jax import lax
from jax.experimental import pallas as pl
from jax.experimental.pallas import tpu as pltpu
from jax.sharding import PartitionSpec as P

sparsity_weight = 4.0
norm_epsilon = 1e-06
TOKENS = 512
D = 4608
HALF = D // 2
AXES = ("prod", "sae")
STEP = 768
VMEM = pltpu.VMEM
bf16 = jnp.bfloat16
f32 = jnp.float32


def place(x, y, z, c):
    return ((y % 2) * 2 + c) * 32 + (x * 4 + z) * 2 + y // 2


def route(step):
    pairs = []
    for x in range(4):
        for y in range(4):
            for z in range(4):
                for c in range(2):
                    tx, ty, tz, tc = step(x, y, z, c)
                    pairs.append((place(x, y, z, c), place(tx % 4, ty % 4, tz % 4, tc % 2)))
    return pairs


def move(value, step):
    return lax.ppermute(value, AXES, route(step))


def to_core(value):
    return move(value, lambda x, y, z, c: (x, y, z, 1 - c))


def to_major(value, d):
    return move(value, lambda x, y, z, c: (x + d, y, z, c) if c == 0 else (x, y, z + d, c))


def to_middle(value, d):
    return move(value, lambda x, y, z, c: (x, y + d, z, c))


def to_minor(value, d):
    return move(value, lambda x, y, z, c: (x, y, z + d, c) if c == 0 else (x + d, y, z, c))


def gather(value, to):
    return [value] + [to(value, -d) for d in (1, 2, 3)]


def swap_blocks(value):
    return value.reshape(4, 4, 32, value.shape[-1]).transpose(1, 0, 2, 3).reshape(value.shape)


def cut_kernel(axis, half_ref, after_ref, weight_ref, out_ref, sems):
    start, rows = half_ref[0] * HALF, out_ref.shape[0] // 4
    copies = []
    for i in range(4):
        if axis == 0:
            part = weight_ref.at[pl.ds(pl.multiple_of(start + i * rows, rows), rows), :]
        else:
            part = weight_ref.at[pl.ds(i * rows, rows), pl.ds(pl.multiple_of(start, HALF), HALF)]
        out = out_ref.at[pl.ds(i * rows, rows), :]
        copies.append(pltpu.make_async_copy(part, out, sems.at[i]))
        copies[-1].start()
    for copy in copies:
        copy.wait()


def cut(weight, axis, half, after):
    shape = (HALF, weight.shape[1]) if axis == 0 else (weight.shape[0], HALF)
    ins = [(half, pltpu.SMEM), (after, None), (weight, None)]
    kernel = functools.partial(cut_kernel, axis)
    scratch = [pltpu.SemaphoreType.DMA((4,))]
    return call(kernel, [(shape, bf16, VMEM)], ins, scratch, 4, 0, weight.size * 2)[0]


def call(kernel, outs, ins, scratch, mib, flops, data, **more):
    def spec(space):
        return pl.BlockSpec(memory_space=pl.ANY if space is None else space)

    return pl.pallas_call(
        kernel,
        out_shape=tuple(jax.ShapeDtypeStruct(shape, dtype) for shape, dtype, _ in outs),
        in_specs=[spec(space) for _, space in ins],
        out_specs=tuple(spec(space) for *_, space in outs),
        scratch_shapes=scratch,
        compiler_params=pltpu.CompilerParams(vmem_limit_bytes=mib * 2**20),
        cost_estimate=pl.CostEstimate(flops=flops, bytes_accessed=data, transcendentals=0),
        **more,
    )(*(value for value, _ in ins))


def flip_kernel(*refs):
    pieces, squares, (_, out, *square_outs) = refs[:4], refs[4:6], refs[6:]
    for k, piece in enumerate(pieces):

        def tile(j, carry, piece=piece, column=128 * k):
            rows = pl.ds(pl.multiple_of(j * 256, 256), 256)
            out[rows, column : column + 128] = piece[:, rows].T
            return carry

        lax.fori_loop(0, HALF // 256, tile, 0)
    for square, square_out in zip(squares, square_outs):
        for i in range(4):
            square_out[:, 128 * i : 128 * i + 128] = square[128 * i : 128 * i + 128, :].T


def flip(pieces, squares, after):
    ins = [(v, VMEM) for v in pieces + squares] + [(after, None)]
    outs = [((HALF, TOKENS), bf16, VMEM)] + [((TOKENS, TOKENS), bf16, VMEM)] * 2
    return call(flip_kernel, outs, ins, [], 8, 0, 6 * 2**20)


def rows_kernel(core, _, weight, act, own, other, factor, penalty, sems):
    copies = []
    for k, out in enumerate((own, other)):
        half = core[0] if k == 0 else 1 - core[0]
        for i in range(4):
            span = slice(128 * i, 128 * i + 128)
            columns = pl.ds(pl.multiple_of(half * HALF, HALF), HALF)
            copies.append(
                pltpu.make_async_copy(
                    weight.at[span, columns], out.at[span, :], sems.at[k, i]
                )
            )
            copies[-1].start()
    for copy in copies:
        copy.wait()
    squares = jnp.zeros((TOKENS, 128), f32)
    for out in (own, other):
        for j in range(HALF // 128):
            wide = out[:, 128 * j : 128 * j + 128].astype(f32)
            squares = squares + wide * wide
    norms = jnp.sqrt(jnp.sum(squares, axis=1, keepdims=True) + norm_epsilon)
    act_sum = jnp.sum(act[...].astype(f32), axis=1, keepdims=True)
    factor[...] = sparsity_weight / TOKENS * (act_sum / norms)
    norms = jnp.broadcast_to(sparsity_weight * norms / TOKENS, (TOKENS, 128))
    penalty[...] = norms.T[:1, :]


def decoder_rows(core, after, weight, act):
    ins = [(core, pltpu.SMEM), (after, None), (weight, None), (act, VMEM)]
    outs = [((TOKENS, HALF), bf16, VMEM)] * 2
    outs += [((TOKENS, 1), f32, VMEM), ((1, TOKENS), f32, VMEM)]
    scratch = [pltpu.SemaphoreType.DMA((2, 4))]
    return call(rows_kernel, outs, ins, scratch, 8, 0, 10 * 2**20)


def times_rows(a, b):
    return lax.dot_general(a, b, (((1,), (1,)), ((), ())), preferred_element_type=f32)


def join(pieces, out):
    for i, piece in enumerate(pieces):
        out[128 * i : 128 * i + 128, :] = piece[...]


def decoder_part(half, out, errors, weight, act, factor, stage, sems):
    copies = []
    for j in range(HALF // STEP):
        span = slice(j * STEP, j * STEP + STEP)
        part = jnp.dot(act[...], errors[:, span], preferred_element_type=f32)
        part = part + factor[...] * weight[:, span].astype(f32)
        stage[j] = part.astype(bf16)
        columns = pl.ds(pl.multiple_of(half * HALF + j * STEP, STEP), STEP)
        copies.append(pltpu.make_async_copy(stage.at[j], out.at[:, columns], sems.at[j]))
        copies[-1].start()
    return copies


def first_kernel(core, *refs):
    pieces, (weight, act, factor, grad_acts, out, errors, stage, sems) = refs[:4], refs[4:]
    join(pieces, errors)
    copies = decoder_part(core[0], out, errors, weight, act, factor, stage, sems)
    total = jnp.zeros((TOKENS, TOKENS), f32)
    for j in range(HALF // STEP):
        span = slice(j * STEP, j * STEP + STEP)
        total = total + times_rows(errors[:, span], weight[:, span])
    grad_acts[...] = total
    for copy in copies:
        copy.wait()


def first_gradients(core, errors, weight, act, factor):
    ins = [(core, pltpu.SMEM)] + [(v, VMEM) for v in [*errors, weight, act, factor]]
    outs = [((TOKENS, TOKENS), f32, VMEM), ((TOKENS, D), bf16, None)]
    scratch = [
        pltpu.VMEM((TOKENS, HALF), bf16),
        pltpu.VMEM((HALF // STEP, TOKENS, STEP), bf16),
        pltpu.SemaphoreType.DMA((HALF // STEP,)),
    ]
    flops = 4 * TOKENS * TOKENS * HALF
    return call(first_kernel, outs, ins, scratch, 24, flops, 8 * 2**20)


def last_kernel(core, _, own_acts, *refs):
    pieces, refs = refs[:4], refs[4:]
    (weight, act, factor, penalty, rectified, flipped_own, flipped_mate) = refs[:7]
    (out, out_encoder, out_bias) = refs[7:10]
    (errors, stage, turned, grads, grads_mate, encoder_stage, sems, encoder_sems) = refs[10:18]
    (streams, stream_sems) = refs[18:]
    loads = []
    for k, flipped in enumerate((flipped_own, flipped_mate)):
        for j in range(HALF // STEP):
            slot = k * (HALF // STEP) + j
            rows = slice(j * STEP, j * STEP + STEP)
            loads.append(
                pltpu.make_async_copy(flipped.at[rows, :], streams.at[slot], stream_sems.at[slot])
            )
            loads[-1].start()
    join(pieces, errors)
    total = jnp.zeros((TOKENS, TOKENS), f32)
    for j in range(HALF // STEP):
        span = slice(j * STEP, j * STEP + STEP)
        total = total + times_rows(errors[:, span], weight[:, span])
    turned[...] = total
    bias = jnp.zeros((1, TOKENS), f32)
    for major in range(4):
        for minor in range(4):
            here, there = (major * 4 + minor) * 32, (minor * 4 + major) * 32
            acts = own_acts[here : here + 32, :] + turned[there : there + 32, :] + penalty[...]
            rounded = (acts * 2.0 * rectified[here : here + 32, :]).astype(bf16)
            grads[here : here + 32, :] = rounded
            grads_mate[there : there + 32, :] = rounded
            bias = bias + jnp.sum(rounded.astype(f32), axis=0, keepdims=True)
    out_bias[...] = bias
    copies = []
    for k, grad in enumerate((grads, grads_mate)):
        half = core[0] if k == 0 else 1 - core[0]
        for j in range(HALF // STEP):
            slot = k * (HALF // STEP) + j
            loads[slot].wait()
            part = jnp.dot(streams[slot], grad[...], preferred_element_type=f32)
            encoder_stage[slot] = part.astype(bf16)
            rows = pl.ds(pl.multiple_of(half * HALF + j * STEP, STEP), STEP)
            copies.append(
                pltpu.make_async_copy(
                    encoder_stage.at[slot], out_encoder.at[rows, :], encoder_sems.at[slot]
                )
            )
            copies[-1].start()
    copies += decoder_part(1 - core[0], out, errors, weight, act, factor, stage, sems)
    for copy in copies:
        copy.wait()


def last_gradients(core, grad_decoder, grad_acts, errors, *rest):
    ins = [(core, pltpu.SMEM), (grad_decoder, None), (grad_acts, VMEM)]
    ins += [(v, VMEM) for v in [*errors, *rest[:-2]]] + [(v, None) for v in rest[-2:]]
    outs = [((TOKENS, D), bf16, None), ((D, TOKENS), bf16, None), ((1, TOKENS), f32, VMEM)]
    steps = HALF // STEP
    scratch = [
        pltpu.VMEM((TOKENS, HALF), bf16),
        pltpu.VMEM((steps, TOKENS, STEP), bf16),
        pltpu.VMEM((TOKENS, TOKENS), f32),
        pltpu.VMEM((TOKENS, TOKENS), bf16),
        pltpu.VMEM((TOKENS, TOKENS), bf16),
        pltpu.VMEM((2 * steps, STEP, TOKENS), bf16),
        pltpu.SemaphoreType.DMA((steps,)),
        pltpu.SemaphoreType.DMA((2 * steps,)),
        pltpu.VMEM((2 * steps, STEP, TOKENS), bf16),
        pltpu.SemaphoreType.DMA((2 * steps,)),
    ]
    flops = 8 * TOKENS * TOKENS * HALF
    return call(
        last_kernel, outs, ins, scratch, 32, flops, 16 * 2**20, input_output_aliases={1: 0}
    )


def dot(a, b):
    return jnp.dot(a, b, preferred_element_type=f32)


def local(
    head_outputs,
    out_weight,
    residual_input,
    post_gain,
    encoder_weight,
    encoder_bias,
    decoder_weight,
    decoder_bias,
):
    here = lax.axis_index("prod")
    low = here // 2 == 0
    first = here % 2 == 0

    def own_half(v):
        return jnp.where(first, v[..., :HALF], v[..., HALF:])

    def other_half(v):
        return jnp.where(first, v[..., HALF:], v[..., :HALF])

    core = (here % 2).reshape(1)
    partial_value = dot(head_outputs, out_weight)
    both = own_half(partial_value) + to_core(other_half(partial_value))
    projected = both + lax.ppermute(both, "prod", [(0, 2), (2, 0), (1, 3), (3, 1)])
    squares = jnp.broadcast_to(jnp.sum(projected * projected, axis=1, keepdims=True), (16, 128))
    squares = (squares + to_core(squares))[:, :1]
    gain = own_half(post_gain)
    normed = projected * lax.rsqrt(squares / D + norm_epsilon) * gain
    stream = (own_half(residual_input).astype(f32) + normed).astype(bf16)

    stream, encoder_send, decoder_send = lax.optimization_barrier(
        (stream, encoder_weight, decoder_weight)
    )
    encoder_mate = to_core(encoder_send)
    decoder_mate = to_core(decoder_send)
    bias_own = own_half(decoder_bias)
    stream = jnp.concatenate([stream, move(stream, lambda x, y, z, c: (x, 3 - y, z, c))])
    stream = jnp.where(low, stream, jnp.roll(stream, -8, axis=0))
    stream = jnp.concatenate(gather(stream, to_minor))
    own_stream = stream.reshape(4, 4, 8, HALF)[:, 0].reshape(32, HALF)
    centred = (stream.astype(f32) - bias_own).astype(bf16)
    centred, encoder_mate, decoder_mate = lax.optimization_barrier(
        (centred, encoder_mate, decoder_mate)
    )
    encoder_mate = cut(encoder_mate, 0, core, centred)
    decoder_mate = cut(decoder_mate, 1, core, centred)
    encoder_own = cut(encoder_weight, 0, core, centred)
    decoder_own = cut(decoder_weight, 1, core, centred)
    centred = gather(centred, to_major)

    for_mate = swap_blocks(jnp.concatenate([dot(piece, encoder_mate) for piece in centred]))
    for_mate, decoder_own, decoder_mate = lax.optimization_barrier(
        (for_mate, decoder_own, decoder_mate)
    )
    preact = jnp.concatenate([dot(piece, encoder_own) for piece in centred])
    preact = preact + to_core(for_mate) + encoder_bias
    rectified = jnp.maximum(preact, 0.0)
    activations = jnp.square(rectified).astype(bf16)
    swapped = swap_blocks(activations)
    mate_activations = to_core(swapped)

    pieces = []
    for d in range(4):
        rows = slice(128 * d, 128 * d + 128)
        piece = dot(activations[rows], decoder_own) + dot(mate_activations[rows], decoder_mate)
        pieces.append(to_major(piece.astype(bf16), d) if d else piece)
    recon = sum(piece.astype(f32) for piece in pieces).astype(bf16)
    flipped_own, flipped_act, flipped_swapped = flip(centred, [activations, swapped], activations)
    recon, flipped_own = lax.optimization_barrier((recon, flipped_own))
    flipped_mate = to_core(flipped_own)
    pieces = [recon.reshape(4, 4, 8, HALF)[:, d].reshape(32, HALF) for d in range(4)]
    pieces = [to_middle(piece, d) if d else piece for d, piece in enumerate(pieces)]
    recon = sum(piece.astype(f32) for piece in pieces).astype(bf16)
    summed = recon.astype(f32)
    for d in (1, 2, 3):
        summed = summed + jnp.roll(to_minor(recon, -d), 8 * d, axis=0).astype(f32)
    grad_recon = (2.0 * (summed + bias_own - own_stream.astype(f32)) / TOKENS).astype(bf16)

    errors = [piece.reshape(4, 1, 8, HALF) for piece in gather(grad_recon, to_middle)]
    errors = jnp.concatenate(errors, axis=1).reshape(128, HALF)
    errors, flipped_mate = lax.optimization_barrier((errors, flipped_mate))
    decoder_own, decoder_other, factor, penalty = decoder_rows(
        core, errors, decoder_weight, flipped_act
    )
    errors = gather(errors, to_major)
    errors[3], decoder_own, decoder_other, factor, penalty = lax.optimization_barrier(
        (errors[3], decoder_own, decoder_other, factor, penalty)
    )
    errors_mate = [to_core(piece) for piece in errors]

    grad_acts, grad_decoder = first_gradients(core, errors, decoder_own, flipped_act, factor)
    grad_decoder, grad_encoder, grad_bias = last_gradients(
        core, grad_decoder, grad_acts, errors_mate, decoder_other, flipped_swapped, factor,
        penalty, rectified, flipped_own, flipped_mate,
    )
    return (grad_encoder, grad_bias.reshape(TOKENS), grad_decoder)


def solution(mesh):
    placed = (
        P("sae", "prod"),
        P("prod", None),
        P("sae", None),
        P(),
        P(None, ("prod", "sae")),
        P(("prod", "sae")),
        P(("prod", "sae"), None),
        P(),
    )
    return jax.shard_map(
        local,
        mesh=mesh,
        in_specs=placed,
        out_specs=(P(None, ("prod", "sae")), P(("prod", "sae")), P(("prod", "sae"), None)),
        check_vma=False,
    )
```

```python
import functools

import jax
import jax.numpy as jnp
from jax import lax
from jax.experimental import pallas as pl
from jax.experimental.pallas import tpu as pltpu
from jax.sharding import PartitionSpec as P

sparsity_weight = 4.0
norm_epsilon = 1e-06
TOKENS = 512
D = 4608
HALF = D // 2
AXES = ("prod", "sae")
STEP = 768
VMEM = pltpu.VMEM
bf16 = jnp.bfloat16
f32 = jnp.float32


def place(x, y, z, c):
    return ((y % 2) * 2 + c) * 32 + (x * 4 + z) * 2 + y // 2


def route(step):
    pairs = []
    for x in range(4):
        for y in range(4):
            for z in range(4):
                for c in range(2):
                    tx, ty, tz, tc = step(x, y, z, c)
                    pairs.append((place(x, y, z, c), place(tx % 4, ty % 4, tz % 4, tc % 2)))
    return pairs


def move(value, step):
    return lax.ppermute(value, AXES, route(step))


def to_core(value):
    return move(value, lambda x, y, z, c: (x, y, z, 1 - c))


def to_major(value, d):
    return move(value, lambda x, y, z, c: (x + d, y, z, c) if c == 0 else (x, y, z + d, c))


def to_y(value, mask):
    return move(value, lambda x, y, z, c: (x, y ^ mask, z, c))


def to_minor(value, d):
    return move(value, lambda x, y, z, c: (x, y, z + d, c) if c == 0 else (x + d, y, z, c))


MASKS = (0, 1, 3, 2)


def gather_y(value):
    pieces = [value] + [to_y(value, mask) for mask in MASKS[1:]]
    pieces = [piece.reshape(4, 1, 8, HALF) for piece in pieces]
    return jnp.concatenate(pieces, axis=1).reshape(128, HALF)


def scatter_y(value):
    pieces = [value.reshape(4, 4, 8, HALF)[:, k].reshape(32, HALF) for k in range(4)]
    pieces = pieces[:1] + [to_y(piece, mask) for piece, mask in zip(pieces[1:], MASKS[1:])]
    return sum(piece.astype(f32) for piece in pieces)


def swap_blocks(value):
    return value.reshape(4, 4, 32, value.shape[-1]).transpose(1, 0, 2, 3).reshape(value.shape)


def cut_kernel(axis, half_ref, after_ref, weight_ref, out_ref, sems):
    start, rows = half_ref[0] * HALF, out_ref.shape[0] // 4
    copies = []
    for i in range(4):
        if axis == 0:
            part = weight_ref.at[pl.ds(pl.multiple_of(start + i * rows, rows), rows), :]
        else:
            part = weight_ref.at[pl.ds(i * rows, rows), pl.ds(pl.multiple_of(start, HALF), HALF)]
        out = out_ref.at[pl.ds(i * rows, rows), :]
        copies.append(pltpu.make_async_copy(part, out, sems.at[i]))
        copies[-1].start()
    for copy in copies:
        copy.wait()


def cut(weight, axis, half, after):
    shape = (HALF, weight.shape[1]) if axis == 0 else (weight.shape[0], HALF)
    ins = [(half, pltpu.SMEM), (after, None), (weight, None)]
    kernel = functools.partial(cut_kernel, axis)
    scratch = [pltpu.SemaphoreType.DMA((4,))]
    return call(kernel, [(shape, bf16, VMEM)], ins, scratch, 4, 0, weight.size * 2)[0]


def call(kernel, outs, ins, scratch, mib, flops, data, **more):
    def spec(space):
        return pl.BlockSpec(memory_space=pl.ANY if space is None else space)

    return pl.pallas_call(
        kernel,
        out_shape=tuple(jax.ShapeDtypeStruct(shape, dtype) for shape, dtype, _ in outs),
        in_specs=[spec(space) for _, space in ins],
        out_specs=tuple(spec(space) for *_, space in outs),
        scratch_shapes=scratch,
        compiler_params=pltpu.CompilerParams(vmem_limit_bytes=mib * 2**20),
        cost_estimate=pl.CostEstimate(flops=flops, bytes_accessed=data, transcendentals=0),
        **more,
    )(*(value for value, _ in ins))


def flip_kernel(*refs):
    pieces, squares, (_, out, *square_outs) = refs[:4], refs[4:6], refs[6:]
    for k, piece in enumerate(pieces):

        def tile(j, carry, piece=piece, column=128 * k):
            rows = pl.ds(pl.multiple_of(j * 256, 256), 256)
            out[rows, column : column + 128] = piece[:, rows].T
            return carry

        lax.fori_loop(0, HALF // 256, tile, 0)
    for square, square_out in zip(squares, square_outs):
        for i in range(4):
            square_out[:, 128 * i : 128 * i + 128] = square[128 * i : 128 * i + 128, :].T


def flip(pieces, squares, after):
    ins = [(v, VMEM) for v in pieces + squares] + [(after, None)]
    outs = [((HALF, TOKENS), bf16, VMEM)] + [((TOKENS, TOKENS), bf16, VMEM)] * 2
    return call(flip_kernel, outs, ins, [], 8, 0, 6 * 2**20)


def rows_kernel(core, _, weight, own, act, other, factor, penalty, sems):
    columns = pl.ds(pl.multiple_of((1 - core[0]) * HALF, HALF), HALF)
    copies = []
    for i in range(4):
        span = slice(128 * i, 128 * i + 128)
        copies.append(
            pltpu.make_async_copy(weight.at[span, columns], other.at[span, :], sems.at[i])
        )
        copies[-1].start()
    squares = jnp.zeros((TOKENS, 128), f32)
    for part in (own, other):
        if part is other:
            for copy in copies:
                copy.wait()
        for j in range(HALF // 128):
            wide = part[:, 128 * j : 128 * j + 128].astype(f32)
            squares = squares + wide * wide
    norms = jnp.sqrt(jnp.sum(squares, axis=1, keepdims=True) + norm_epsilon)
    act_sum = jnp.sum(act[...].astype(f32), axis=1, keepdims=True)
    factor[...] = sparsity_weight / TOKENS * (act_sum / norms)
    norms = jnp.broadcast_to(sparsity_weight * norms / TOKENS, (TOKENS, 128))
    penalty[...] = norms.T[:1, :]


def decoder_rows(core, after, weight, own, act):
    ins = [(core, pltpu.SMEM), (after, None), (weight, None), (own, VMEM), (act, VMEM)]
    outs = [((TOKENS, HALF), bf16, VMEM)]
    outs += [((TOKENS, 1), f32, VMEM), ((1, TOKENS), f32, VMEM)]
    scratch = [pltpu.SemaphoreType.DMA((4,))]
    return call(rows_kernel, outs, ins, scratch, 8, 0, 6 * 2**20)


def times_rows(a, b):
    return lax.dot_general(a, b, (((1,), (1,)), ((), ())), preferred_element_type=f32)


def join(pieces, out):
    for i, piece in enumerate(pieces):
        out[128 * i : 128 * i + 128, :] = piece[...]


def decoder_part(half, out, errors, weight, act, factor, stage, sems):
    copies = []
    for j in range(HALF // STEP):
        span = slice(j * STEP, j * STEP + STEP)
        part = jnp.dot(act[...], errors[:, span], preferred_element_type=f32)
        part = part + factor[...] * weight[:, span].astype(f32)
        stage[j] = part.astype(bf16)
        columns = pl.ds(pl.multiple_of(half * HALF + j * STEP, STEP), STEP)
        copies.append(pltpu.make_async_copy(stage.at[j], out.at[:, columns], sems.at[j]))
        copies[-1].start()
    return copies


def first_kernel(core, *refs):
    pieces, (weight, act, factor, grad_acts, out, errors, stage, sems) = refs[:4], refs[4:]
    join(pieces, errors)
    copies = decoder_part(core[0], out, errors, weight, act, factor, stage, sems)
    total = jnp.zeros((TOKENS, TOKENS), f32)
    for j in range(HALF // STEP):
        span = slice(j * STEP, j * STEP + STEP)
        total = total + times_rows(errors[:, span], weight[:, span])
    grad_acts[...] = total
    for copy in copies:
        copy.wait()


def first_gradients(core, errors, weight, act, factor):
    ins = [(core, pltpu.SMEM)] + [(v, VMEM) for v in [*errors, weight, act, factor]]
    outs = [((TOKENS, TOKENS), f32, VMEM), ((TOKENS, D), bf16, None)]
    scratch = [
        pltpu.VMEM((TOKENS, HALF), bf16),
        pltpu.VMEM((HALF // STEP, TOKENS, STEP), bf16),
        pltpu.SemaphoreType.DMA((HALF // STEP,)),
    ]
    flops = 4 * TOKENS * TOKENS * HALF
    return call(first_kernel, outs, ins, scratch, 24, flops, 8 * 2**20)


def last_kernel(core, _, own_acts, *refs):
    pieces, refs = refs[:4], refs[4:]
    (weight, act, factor, penalty, rectified, flipped_own, flipped_mate) = refs[:7]
    (out, out_encoder, out_bias) = refs[7:10]
    (errors, stage, turned, grads, grads_mate, encoder_stage, sems, encoder_sems) = refs[10:18]
    (streams, stream_sems) = refs[18:]
    loads = []
    for k, flipped in enumerate((flipped_own, flipped_mate)):
        for j in range(HALF // STEP):
            slot = k * (HALF // STEP) + j
            rows = slice(j * STEP, j * STEP + STEP)
            loads.append(
                pltpu.make_async_copy(flipped.at[rows, :], streams.at[slot], stream_sems.at[slot])
            )
            loads[-1].start()
    join(pieces, errors)
    total = jnp.zeros((TOKENS, TOKENS), f32)
    for j in range(HALF // STEP):
        span = slice(j * STEP, j * STEP + STEP)
        total = total + times_rows(errors[:, span], weight[:, span])
    turned[...] = total
    bias = jnp.zeros((1, TOKENS), f32)
    for major in range(4):
        for minor in range(4):
            here, there = (major * 4 + minor) * 32, (minor * 4 + major) * 32
            acts = own_acts[here : here + 32, :] + turned[there : there + 32, :] + penalty[...]
            rounded = (acts * 2.0 * rectified[here : here + 32, :]).astype(bf16)
            grads[here : here + 32, :] = rounded
            grads_mate[there : there + 32, :] = rounded
            bias = bias + jnp.sum(rounded.astype(f32), axis=0, keepdims=True)
    out_bias[...] = bias
    copies = []
    for k, grad in enumerate((grads, grads_mate)):
        half = core[0] if k == 0 else 1 - core[0]
        for j in range(HALF // STEP):
            slot = k * (HALF // STEP) + j
            loads[slot].wait()
            part = jnp.dot(streams[slot], grad[...], preferred_element_type=f32)
            encoder_stage[slot] = part.astype(bf16)
            rows = pl.ds(pl.multiple_of(half * HALF + j * STEP, STEP), STEP)
            copies.append(
                pltpu.make_async_copy(
                    encoder_stage.at[slot], out_encoder.at[rows, :], encoder_sems.at[slot]
                )
            )
            copies[-1].start()
    copies += decoder_part(1 - core[0], out, errors, weight, act, factor, stage, sems)
    for copy in copies:
        copy.wait()


def last_gradients(core, grad_decoder, grad_acts, errors, *rest):
    ins = [(core, pltpu.SMEM), (grad_decoder, None), (grad_acts, VMEM)]
    ins += [(v, VMEM) for v in [*errors, *rest[:-2]]] + [(v, None) for v in rest[-2:]]
    outs = [((TOKENS, D), bf16, None), ((D, TOKENS), bf16, None), ((1, TOKENS), f32, VMEM)]
    steps = HALF // STEP
    scratch = [
        pltpu.VMEM((TOKENS, HALF), bf16),
        pltpu.VMEM((steps, TOKENS, STEP), bf16),
        pltpu.VMEM((TOKENS, TOKENS), f32),
        pltpu.VMEM((TOKENS, TOKENS), bf16),
        pltpu.VMEM((TOKENS, TOKENS), bf16),
        pltpu.VMEM((2 * steps, STEP, TOKENS), bf16),
        pltpu.SemaphoreType.DMA((steps,)),
        pltpu.SemaphoreType.DMA((2 * steps,)),
        pltpu.VMEM((2 * steps, STEP, TOKENS), bf16),
        pltpu.SemaphoreType.DMA((2 * steps,)),
    ]
    flops = 8 * TOKENS * TOKENS * HALF
    return call(
        last_kernel, outs, ins, scratch, 32, flops, 16 * 2**20, input_output_aliases={1: 0}
    )


def dot(a, b):
    return jnp.dot(a, b, preferred_element_type=f32)


def local(
    head_outputs,
    out_weight,
    residual_input,
    post_gain,
    encoder_weight,
    encoder_bias,
    decoder_weight,
    decoder_bias,
):
    here = lax.axis_index("prod")
    low = here // 2 == 0
    first = here % 2 == 0

    def own_half(v):
        return jnp.where(first, v[..., :HALF], v[..., HALF:])

    def other_half(v):
        return jnp.where(first, v[..., HALF:], v[..., :HALF])

    core = (here % 2).reshape(1)
    partial_value = dot(head_outputs, out_weight)
    both = own_half(partial_value) + to_core(other_half(partial_value))
    projected = both + lax.ppermute(both, "prod", [(0, 2), (2, 0), (1, 3), (3, 1)])
    squares = jnp.broadcast_to(jnp.sum(projected * projected, axis=1, keepdims=True), (16, 128))
    squares = (squares + to_core(squares))[:, :1]
    gain = own_half(post_gain)
    normed = projected * lax.rsqrt(squares / D + norm_epsilon) * gain
    stream = (own_half(residual_input).astype(f32) + normed).astype(bf16)
    stream = jnp.where(low, stream, jnp.roll(stream, 8, axis=0))

    stream, encoder_send, decoder_send = lax.optimization_barrier(
        (stream, encoder_weight, decoder_weight)
    )
    encoder_mate = to_core(encoder_send)
    decoder_mate = to_core(decoder_send)
    bias_own = own_half(decoder_bias)
    stream = jnp.concatenate([stream, to_y(stream, 3)])
    stream = jnp.concatenate([stream] + [to_minor(stream, -d) for d in (1, 2, 3)])
    own_stream = stream.reshape(4, 4, 8, HALF)[:, 0].reshape(32, HALF)
    centred = (stream.astype(f32) - bias_own).astype(bf16)
    centred, encoder_mate, decoder_mate = lax.optimization_barrier(
        (centred, encoder_mate, decoder_mate)
    )
    encoder_mate = cut(encoder_mate, 0, core, centred)
    decoder_mate = cut(decoder_mate, 1, core, centred)
    encoder_own = cut(encoder_weight, 0, core, centred)
    decoder_own = cut(decoder_weight, 1, core, centred)
    centred = [centred] + [to_major(centred, -d) for d in (1, 2, 3)]

    for_mate = swap_blocks(jnp.concatenate([dot(piece, encoder_mate) for piece in centred]))
    for_mate, decoder_own, decoder_mate = lax.optimization_barrier(
        (for_mate, decoder_own, decoder_mate)
    )
    preact = jnp.concatenate([dot(piece, encoder_own) for piece in centred])
    preact = preact + to_core(for_mate) + encoder_bias
    rectified = jnp.maximum(preact, 0.0)
    activations = jnp.square(rectified).astype(bf16)
    swapped = swap_blocks(activations)
    mate_activations = to_core(swapped)

    pieces = {}
    for d in range(4):
        rows = slice(128 * d, 128 * d + 128)
        own = dot(activations[rows], decoder_own)
        pieces[d] = (own + dot(mate_activations[rows], decoder_mate)).astype(bf16)
    far = pieces[2].reshape(4, 4, 8, HALF)
    keep = jnp.where(first, far[:, :2], far[:, ::2])
    send = jnp.where(first, far[:, 2:], far[:, 1::2])
    send = move(send, lambda x, y, z, c: (x, y ^ (3 if c == 0 else 1), z, c))
    far = (keep.astype(f32) + send.astype(f32)).astype(bf16)
    send = move(far[:, 1], lambda x, y, z, c: (x, y ^ (1 if c == 0 else 3), z, c))
    far = (far[:, 0].astype(f32) + send.astype(f32)).astype(bf16).reshape(32, HALF)
    recon = [pieces[0], to_major(pieces[1], 1), to_major(pieces[3], 3)]
    recon = sum(piece.astype(f32) for piece in recon).astype(bf16)
    flipped_own, flipped_act, flipped_swapped = flip(centred, [activations, swapped], pieces[0])
    decoder_other, factor, penalty = decoder_rows(
        core, pieces[0], decoder_weight, decoder_own, flipped_act
    )
    recon, flipped_own, decoder_other, factor, penalty = lax.optimization_barrier(
        (recon, flipped_own, decoder_other, factor, penalty)
    )
    flipped_mate = to_core(flipped_own)
    recon = (scatter_y(recon) + to_major(far, 2).astype(f32)).astype(bf16)
    summed = recon.astype(f32)
    for d in (1, 2, 3):
        summed = summed + jnp.roll(to_minor(recon, -d), 8 * d, axis=0).astype(f32)
    grad_recon = (2.0 * (summed + bias_own - own_stream.astype(f32)) / TOKENS).astype(bf16)

    far = to_major(grad_recon, 2)
    errors = gather_y(grad_recon)
    errors, flipped_mate = lax.optimization_barrier((errors, flipped_mate))
    errors = [errors, to_major(errors, -1), gather_y(far), to_major(errors, -3)]
    errors_mate = [to_core(piece) for piece in errors]

    grad_acts, grad_decoder = first_gradients(core, errors, decoder_own, flipped_act, factor)
    grad_decoder, grad_encoder, grad_bias = last_gradients(
        core, grad_decoder, grad_acts, errors_mate, decoder_other, flipped_swapped, factor,
        penalty, rectified, flipped_own, flipped_mate,
    )
    return (grad_encoder, grad_bias.reshape(TOKENS), grad_decoder)


def solution(mesh):
    placed = (
        P("sae", "prod"),
        P("prod", None),
        P("sae", None),
        P(),
        P(None, ("prod", "sae")),
        P(("prod", "sae")),
        P(("prod", "sae"), None),
        P(),
    )
    return jax.shard_map(
        local,
        mesh=mesh,
        in_specs=placed,
        out_specs=(P(None, ("prod", "sae")), P(("prod", "sae")), P(("prod", "sae"), None)),
        check_vma=False,
    )
```

```python
import functools

import jax
import jax.numpy as jnp
from jax import lax
from jax.experimental import pallas as pl
from jax.experimental.pallas import tpu as pltpu
from jax.sharding import PartitionSpec as P

sparsity_weight = 4.0
norm_epsilon = 1e-06
TOKENS = 512
D = 4608
HALF = D // 2
AXES = ("prod", "sae")
STEP = 768
VMEM = pltpu.VMEM
bf16 = jnp.bfloat16
f32 = jnp.float32


def place(x, y, z, c):
    return ((y % 2) * 2 + c) * 32 + (x * 4 + z) * 2 + y // 2


def route(step):
    pairs = []
    for x in range(4):
        for y in range(4):
            for z in range(4):
                for c in range(2):
                    tx, ty, tz, tc = step(x, y, z, c)
                    pairs.append((place(x, y, z, c), place(tx % 4, ty % 4, tz % 4, tc % 2)))
    return pairs


def move(value, step):
    return lax.ppermute(value, AXES, route(step))


def to_core(value):
    return move(value, lambda x, y, z, c: (x, y, z, 1 - c))


def to_major(value, d):
    return move(value, lambda x, y, z, c: (x + d, y, z, c) if c == 0 else (x, y, z + d, c))


def to_y(value, mask):
    return move(value, lambda x, y, z, c: (x, y ^ mask, z, c))


def to_minor(value, d):
    return move(value, lambda x, y, z, c: (x, y, z + d, c) if c == 0 else (x + d, y, z, c))


MASKS = (0, 1, 3, 2)


def gather_y(value):
    pieces = [value] + [to_y(value, mask) for mask in MASKS[1:]]
    pieces = [piece.reshape(4, 1, 8, HALF) for piece in pieces]
    return jnp.concatenate(pieces, axis=1).reshape(128, HALF)


def scatter_y(value):
    pieces = [value.reshape(4, 4, 8, HALF)[:, k].reshape(32, HALF) for k in range(4)]
    pieces = pieces[:1] + [to_y(piece, mask) for piece, mask in zip(pieces[1:], MASKS[1:])]
    return sum(piece.astype(f32) for piece in pieces)


def swap_blocks(value):
    return value.reshape(4, 4, 32, value.shape[-1]).transpose(1, 0, 2, 3).reshape(value.shape)


def cut_kernel(axis, half_ref, after_ref, weight_ref, out_ref, sems):
    start, rows = half_ref[0] * HALF, out_ref.shape[0] // 4
    copies = []
    for i in range(4):
        if axis == 0:
            part = weight_ref.at[pl.ds(pl.multiple_of(start + i * rows, rows), rows), :]
        else:
            part = weight_ref.at[pl.ds(i * rows, rows), pl.ds(pl.multiple_of(start, HALF), HALF)]
        out = out_ref.at[pl.ds(i * rows, rows), :]
        copies.append(pltpu.make_async_copy(part, out, sems.at[i]))
        copies[-1].start()
    for copy in copies:
        copy.wait()


def cut(weight, axis, half, after):
    shape = (HALF, weight.shape[1]) if axis == 0 else (weight.shape[0], HALF)
    ins = [(half, pltpu.SMEM), (after, None), (weight, None)]
    kernel = functools.partial(cut_kernel, axis)
    scratch = [pltpu.SemaphoreType.DMA((4,))]
    return call(kernel, [(shape, bf16, VMEM)], ins, scratch, 4, 0, weight.size * 2)[0]


def call(kernel, outs, ins, scratch, mib, flops, data, **more):
    def spec(space):
        return pl.BlockSpec(memory_space=pl.ANY if space is None else space)

    return pl.pallas_call(
        kernel,
        out_shape=tuple(jax.ShapeDtypeStruct(shape, dtype) for shape, dtype, _ in outs),
        in_specs=[spec(space) for _, space in ins],
        out_specs=tuple(spec(space) for *_, space in outs),
        scratch_shapes=scratch,
        compiler_params=pltpu.CompilerParams(vmem_limit_bytes=mib * 2**20),
        cost_estimate=pl.CostEstimate(flops=flops, bytes_accessed=data, transcendentals=0),
        **more,
    )(*(value for value, _ in ins))


def flip_kernel(*refs):
    pieces, squares, (_, out, *square_outs) = refs[:4], refs[4:6], refs[6:]
    for k, piece in enumerate(pieces):

        def tile(j, carry, piece=piece, column=128 * k):
            rows = pl.ds(pl.multiple_of(j * 256, 256), 256)
            out[rows, column : column + 128] = piece[:, rows].T
            return carry

        lax.fori_loop(0, HALF // 256, tile, 0)
    for square, square_out in zip(squares, square_outs):
        for i in range(4):
            square_out[:, 128 * i : 128 * i + 128] = square[128 * i : 128 * i + 128, :].T


def flip(pieces, squares, after):
    ins = [(v, VMEM) for v in pieces + squares] + [(after, None)]
    outs = [((HALF, TOKENS), bf16, VMEM)] + [((TOKENS, TOKENS), bf16, VMEM)] * 2
    return call(flip_kernel, outs, ins, [], 8, 0, 6 * 2**20)


def rows_kernel(core, _, weight, own, act, other, factor, penalty, sems):
    columns = pl.ds(pl.multiple_of((1 - core[0]) * HALF, HALF), HALF)
    copies = []
    for i in range(4):
        span = slice(128 * i, 128 * i + 128)
        copies.append(
            pltpu.make_async_copy(weight.at[span, columns], other.at[span, :], sems.at[i])
        )
        copies[-1].start()
    squares = jnp.zeros((TOKENS, 128), f32)
    for part in (own, other):
        if part is other:
            for copy in copies:
                copy.wait()
        for j in range(HALF // 128):
            wide = part[:, 128 * j : 128 * j + 128].astype(f32)
            squares = squares + wide * wide
    norms = jnp.sqrt(jnp.sum(squares, axis=1, keepdims=True) + norm_epsilon)
    act_sum = jnp.sum(act[...].astype(f32), axis=1, keepdims=True)
    factor[...] = sparsity_weight / TOKENS * (act_sum / norms)
    norms = jnp.broadcast_to(sparsity_weight * norms / TOKENS, (TOKENS, 128))
    penalty[...] = norms.T[:1, :]


def decoder_rows(core, after, weight, own, act):
    ins = [(core, pltpu.SMEM), (after, None), (weight, None), (own, VMEM), (act, VMEM)]
    outs = [((TOKENS, HALF), bf16, VMEM)]
    outs += [((TOKENS, 1), f32, VMEM), ((1, TOKENS), f32, VMEM)]
    scratch = [pltpu.SemaphoreType.DMA((4,))]
    return call(rows_kernel, outs, ins, scratch, 8, 0, 6 * 2**20)


def times_rows(a, b):
    return lax.dot_general(a, b, (((1,), (1,)), ((), ())), preferred_element_type=f32)


def join(pieces, out):
    for i, piece in enumerate(pieces):
        out[128 * i : 128 * i + 128, :] = piece[...]


def decoder_part(half, out, errors, weight, act, factor, stage, sems):
    copies = []
    for j in range(HALF // STEP):
        span = slice(j * STEP, j * STEP + STEP)
        part = jnp.dot(act[...], errors[:, span], preferred_element_type=f32)
        part = part + factor[...] * weight[:, span].astype(f32)
        stage[j] = part.astype(bf16)
        columns = pl.ds(pl.multiple_of(half * HALF + j * STEP, STEP), STEP)
        copies.append(pltpu.make_async_copy(stage.at[j], out.at[:, columns], sems.at[j]))
        copies[-1].start()
    return copies


def first_kernel(core, *refs):
    pieces, (weight, act, factor, grad_acts, out, errors, stage, sems) = refs[:4], refs[4:]
    join(pieces, errors)
    copies = decoder_part(core[0], out, errors, weight, act, factor, stage, sems)
    total = jnp.zeros((TOKENS, TOKENS), f32)
    for j in range(HALF // STEP):
        span = slice(j * STEP, j * STEP + STEP)
        total = total + times_rows(errors[:, span], weight[:, span])
    grad_acts[...] = total
    for copy in copies:
        copy.wait()


def first_gradients(core, errors, weight, act, factor):
    ins = [(core, pltpu.SMEM)] + [(v, VMEM) for v in [*errors, weight, act, factor]]
    outs = [((TOKENS, TOKENS), f32, VMEM), ((TOKENS, D), bf16, None)]
    scratch = [
        pltpu.VMEM((TOKENS, HALF), bf16),
        pltpu.VMEM((HALF // STEP, TOKENS, STEP), bf16),
        pltpu.SemaphoreType.DMA((HALF // STEP,)),
    ]
    flops = 4 * TOKENS * TOKENS * HALF
    return call(first_kernel, outs, ins, scratch, 24, flops, 8 * 2**20)


def last_kernel(core, _, own_acts, *refs):
    pieces, refs = refs[:4], refs[4:]
    (weight, act, factor, penalty, rectified, flipped_own, flipped_mate) = refs[:7]
    (out, out_encoder, out_bias) = refs[7:10]
    (errors, stage, turned, grads, grads_mate, encoder_stage, sems, encoder_sems) = refs[10:]
    join(pieces, errors)
    turned[...] = times_rows(errors[...], weight[...])
    bias = jnp.zeros((1, TOKENS), f32)
    for major in range(4):
        for minor in range(4):
            here, there = (major * 4 + minor) * 32, (minor * 4 + major) * 32
            acts = own_acts[here : here + 32, :] + turned[there : there + 32, :] + penalty[...]
            rounded = (acts * 2.0 * rectified[here : here + 32, :]).astype(bf16)
            grads[here : here + 32, :] = rounded
            grads_mate[there : there + 32, :] = rounded
            bias = bias + jnp.sum(rounded.astype(f32), axis=0, keepdims=True)
    out_bias[...] = bias
    copies = []
    for k, (flipped, grad) in enumerate(((flipped_own, grads), (flipped_mate, grads_mate))):
        half = core[0] if k == 0 else 1 - core[0]
        for j in range(HALF // STEP):
            slot = k * (HALF // STEP) + j
            part = flipped[j * STEP : j * STEP + STEP, :]
            part = jnp.dot(part, grad[...], preferred_element_type=f32)
            encoder_stage[slot] = part.astype(bf16)
            rows = pl.ds(pl.multiple_of(half * HALF + j * STEP, STEP), STEP)
            copies.append(
                pltpu.make_async_copy(
                    encoder_stage.at[slot], out_encoder.at[rows, :], encoder_sems.at[slot]
                )
            )
            copies[-1].start()
    copies += decoder_part(1 - core[0], out, errors, weight, act, factor, stage, sems)
    for copy in copies:
        copy.wait()


def last_gradients(core, grad_decoder, grad_acts, errors, *rest):
    ins = [(core, pltpu.SMEM), (grad_decoder, None), (grad_acts, VMEM)]
    ins += [(v, VMEM) for v in [*errors, *rest]]
    outs = [((TOKENS, D), bf16, None), ((D, TOKENS), bf16, None), ((1, TOKENS), f32, VMEM)]
    steps = HALF // STEP
    scratch = [
        pltpu.VMEM((TOKENS, HALF), bf16),
        pltpu.VMEM((steps, TOKENS, STEP), bf16),
        pltpu.VMEM((TOKENS, TOKENS), f32),
        pltpu.VMEM((TOKENS, TOKENS), bf16),
        pltpu.VMEM((TOKENS, TOKENS), bf16),
        pltpu.VMEM((2 * steps, STEP, TOKENS), bf16),
        pltpu.SemaphoreType.DMA((steps,)),
        pltpu.SemaphoreType.DMA((2 * steps,)),
    ]
    flops = 8 * TOKENS * TOKENS * HALF
    return call(
        last_kernel, outs, ins, scratch, 32, flops, 16 * 2**20, input_output_aliases={1: 0}
    )


def dot(a, b):
    return jnp.dot(a, b, preferred_element_type=f32)


def local(
    head_outputs,
    out_weight,
    residual_input,
    post_gain,
    encoder_weight,
    encoder_bias,
    decoder_weight,
    decoder_bias,
):
    here = lax.axis_index("prod")
    low = here // 2 == 0
    first = here % 2 == 0

    def own_half(v):
        return jnp.where(first, v[..., :HALF], v[..., HALF:])

    def other_half(v):
        return jnp.where(first, v[..., HALF:], v[..., :HALF])

    core = (here % 2).reshape(1)
    partial_value = dot(head_outputs, out_weight)
    both = own_half(partial_value) + to_core(other_half(partial_value))
    encoder_other = cut(encoder_weight, 0, 1 - core, both)
    decoder_other = cut(decoder_weight, 1, 1 - core, both)
    projected = both + lax.ppermute(both, "prod", [(0, 2), (2, 0), (1, 3), (3, 1)])
    projected, encoder_other, decoder_other = lax.optimization_barrier(
        (projected, encoder_other, decoder_other)
    )
    squares = jnp.broadcast_to(jnp.sum(projected * projected, axis=1, keepdims=True), (16, 128))
    squares = (squares + to_core(squares))[:, :1]
    gain = own_half(post_gain)
    normed = projected * lax.rsqrt(squares / D + norm_epsilon) * gain
    stream = (own_half(residual_input).astype(f32) + normed).astype(bf16)
    stream = jnp.where(low, stream, jnp.roll(stream, 8, axis=0))

    stream, encoder_other, decoder_other = lax.optimization_barrier(
        (stream, encoder_other, decoder_other)
    )
    encoder_mate = to_core(encoder_other)
    decoder_mate = to_core(decoder_other)
    bias_own = own_half(decoder_bias)
    stream = jnp.concatenate([stream, to_y(stream, 3)])
    stream = jnp.concatenate([stream] + [to_minor(stream, -d) for d in (1, 2, 3)])
    own_stream = stream.reshape(4, 4, 8, HALF)[:, 0].reshape(32, HALF)
    centred = (stream.astype(f32) - bias_own).astype(bf16)
    centred, encoder_mate, decoder_mate = lax.optimization_barrier(
        (centred, encoder_mate, decoder_mate)
    )
    encoder_mate = cut(encoder_mate, 0, core * 0, centred)
    decoder_mate = cut(decoder_mate, 1, core * 0, centred)
    encoder_own = cut(encoder_weight, 0, core, centred)
    decoder_own = cut(decoder_weight, 1, core, centred)
    centred = [centred] + [to_major(centred, -d) for d in (1, 2, 3)]

    for_mate = swap_blocks(jnp.concatenate([dot(piece, encoder_mate) for piece in centred]))
    for_mate, decoder_own, decoder_mate = lax.optimization_barrier(
        (for_mate, decoder_own, decoder_mate)
    )
    preact = jnp.concatenate([dot(piece, encoder_own) for piece in centred])
    preact = preact + to_core(for_mate) + encoder_bias
    rectified = jnp.maximum(preact, 0.0)
    activations = jnp.square(rectified).astype(bf16)
    swapped = swap_blocks(activations)
    mate_activations = to_core(swapped)

    pieces = {}
    for d in range(4):
        rows = slice(128 * d, 128 * d + 128)
        own = dot(activations[rows], decoder_own)
        pieces[d] = (own + dot(mate_activations[rows], decoder_mate)).astype(bf16)
    far = pieces[2].reshape(4, 4, 8, HALF)
    keep = jnp.where(first, far[:, :2], far[:, ::2])
    send = jnp.where(first, far[:, 2:], far[:, 1::2])
    send = move(send, lambda x, y, z, c: (x, y ^ (3 if c == 0 else 1), z, c))
    far = (keep.astype(f32) + send.astype(f32)).astype(bf16)
    send = move(far[:, 1], lambda x, y, z, c: (x, y ^ (1 if c == 0 else 3), z, c))
    far = (far[:, 0].astype(f32) + send.astype(f32)).astype(bf16).reshape(32, HALF)
    recon = [pieces[0], to_major(pieces[1], 1), to_major(pieces[3], 3)]
    recon = sum(piece.astype(f32) for piece in recon).astype(bf16)
    flipped_own, flipped_act, flipped_swapped = flip(centred, [activations, swapped], pieces[0])
    decoder_other, factor, penalty = decoder_rows(
        core, pieces[0], decoder_weight, decoder_own, flipped_act
    )
    recon, flipped_own, decoder_other, factor, penalty = lax.optimization_barrier(
        (recon, flipped_own, decoder_other, factor, penalty)
    )
    flipped_mate = to_core(flipped_own)
    recon = (scatter_y(recon) + to_major(far, 2).astype(f32)).astype(bf16)
    summed = recon.astype(f32)
    for d in (1, 2, 3):
        summed = summed + jnp.roll(to_minor(recon, -d), 8 * d, axis=0).astype(f32)
    grad_recon = (2.0 * (summed + bias_own - own_stream.astype(f32)) / TOKENS).astype(bf16)

    far = to_major(grad_recon, 2)
    errors = gather_y(grad_recon)
    errors, flipped_mate = lax.optimization_barrier((errors, flipped_mate))
    errors = [errors, to_major(errors, -1), gather_y(far), to_major(errors, -3)]
    errors_mate = [to_core(piece) for piece in errors]

    grad_acts, grad_decoder = first_gradients(core, errors, decoder_own, flipped_act, factor)
    grad_decoder, grad_encoder, grad_bias = last_gradients(
        core, grad_decoder, grad_acts, errors_mate, decoder_other, flipped_swapped, factor,
        penalty, rectified, flipped_own, flipped_mate,
    )
    return (grad_encoder, grad_bias.reshape(TOKENS), grad_decoder)


def solution(mesh):
    placed = (
        P("sae", "prod"),
        P("prod", None),
        P("sae", None),
        P(),
        P(None, ("prod", "sae")),
        P(("prod", "sae")),
        P(("prod", "sae"), None),
        P(),
    )
    return jax.shard_map(
        local,
        mesh=mesh,
        in_specs=placed,
        out_specs=(P(None, ("prod", "sae")), P(("prod", "sae")), P(("prod", "sae"), None)),
        check_vma=False,
    )
```

```python
import functools

import jax
import jax.numpy as jnp
from jax import lax
from jax.experimental import pallas as pl
from jax.experimental.pallas import tpu as pltpu
from jax.sharding import PartitionSpec as P

sparsity_weight = 4.0
norm_epsilon = 1e-06
TOKENS = 512
D = 4608
HALF = D // 2
AXES = ("prod", "sae")
STEP = 768
VMEM = pltpu.VMEM
bf16 = jnp.bfloat16
f32 = jnp.float32


def place(x, y, z, c):
    return ((y % 2) * 2 + c) * 32 + (x * 4 + z) * 2 + y // 2


def route(step):
    pairs = []
    for x in range(4):
        for y in range(4):
            for z in range(4):
                for c in range(2):
                    tx, ty, tz, tc = step(x, y, z, c)
                    pairs.append((place(x, y, z, c), place(tx % 4, ty % 4, tz % 4, tc % 2)))
    return pairs


def move(value, step):
    return lax.ppermute(value, AXES, route(step))


def to_core(value):
    return move(value, lambda x, y, z, c: (x, y, z, 1 - c))


def to_major(value, d):
    return move(value, lambda x, y, z, c: (x + d, y, z, c) if c == 0 else (x, y, z + d, c))


def to_y(value, mask):
    return move(value, lambda x, y, z, c: (x, y ^ mask, z, c))


def to_minor(value, d):
    return move(value, lambda x, y, z, c: (x, y, z + d, c) if c == 0 else (x + d, y, z, c))


MASKS = (0, 1, 3, 2)


def gather_y(value):
    pieces = [value] + [to_y(value, mask) for mask in MASKS[1:]]
    pieces = [piece.reshape(4, 1, 8, HALF) for piece in pieces]
    return jnp.concatenate(pieces, axis=1).reshape(128, HALF)


def scatter_y(value):
    pieces = [value.reshape(4, 4, 8, HALF)[:, k].reshape(32, HALF) for k in range(4)]
    pieces = pieces[:1] + [to_y(piece, mask) for piece, mask in zip(pieces[1:], MASKS[1:])]
    return sum(piece.astype(f32) for piece in pieces)


def swap_blocks(value):
    return value.reshape(4, 4, 32, value.shape[-1]).transpose(1, 0, 2, 3).reshape(value.shape)


def product_kernel(a, b, out):
    for j in range(HALF // STEP):
        span = slice(j * STEP, j * STEP + STEP)
        out[:, span] = jnp.dot(a[...], b[:, span], preferred_element_type=f32)


def product(a, b):
    outs = [((a.shape[0], b.shape[1]), f32, VMEM)]
    return call(product_kernel, outs, [(a, VMEM), (b, VMEM)], [], 12, 1024, 1024)[0]


def cut_kernel(axis, half_ref, after_ref, weight_ref, out_ref, sems):
    start, rows = half_ref[0] * HALF, out_ref.shape[0] // 4
    copies = []
    for i in range(4):
        if axis == 0:
            part = weight_ref.at[pl.ds(pl.multiple_of(start + i * rows, rows), rows), :]
        else:
            part = weight_ref.at[pl.ds(i * rows, rows), pl.ds(pl.multiple_of(start, HALF), HALF)]
        out = out_ref.at[pl.ds(i * rows, rows), :]
        copies.append(pltpu.make_async_copy(part, out, sems.at[i]))
        copies[-1].start()
    for copy in copies:
        copy.wait()


def cut(weight, axis, half, after):
    shape = (HALF, weight.shape[1]) if axis == 0 else (weight.shape[0], HALF)
    ins = [(half, pltpu.SMEM), (after, None), (weight, None)]
    kernel = functools.partial(cut_kernel, axis)
    scratch = [pltpu.SemaphoreType.DMA((4,))]
    return call(kernel, [(shape, bf16, VMEM)], ins, scratch, 4, 0, weight.size * 2)[0]


def call(kernel, outs, ins, scratch, mib, flops, data, **more):
    def spec(space):
        return pl.BlockSpec(memory_space=pl.ANY if space is None else space)

    return pl.pallas_call(
        kernel,
        out_shape=tuple(jax.ShapeDtypeStruct(shape, dtype) for shape, dtype, _ in outs),
        in_specs=[spec(space) for _, space in ins],
        out_specs=tuple(spec(space) for *_, space in outs),
        scratch_shapes=scratch,
        compiler_params=pltpu.CompilerParams(vmem_limit_bytes=mib * 2**20),
        cost_estimate=pl.CostEstimate(flops=flops, bytes_accessed=data, transcendentals=0),
        **more,
    )(*(value for value, _ in ins))


def flip_kernel(*refs):
    pieces, squares, (_, out, *square_outs) = refs[:4], refs[4:6], refs[6:]
    for k, piece in enumerate(pieces):

        def tile(j, carry, piece=piece, column=128 * k):
            rows = pl.ds(pl.multiple_of(j * 256, 256), 256)
            out[rows, column : column + 128] = piece[:, rows].T
            return carry

        lax.fori_loop(0, HALF // 256, tile, 0)
    for square, square_out in zip(squares, square_outs):
        for i in range(4):
            square_out[:, 128 * i : 128 * i + 128] = square[128 * i : 128 * i + 128, :].T


def flip(pieces, squares, after):
    ins = [(v, VMEM) for v in pieces + squares] + [(after, None)]
    outs = [((HALF, TOKENS), bf16, VMEM)] + [((TOKENS, TOKENS), bf16, VMEM)] * 2
    return call(flip_kernel, outs, ins, [], 8, 0, 6 * 2**20)


def rows_kernel(core, _, weight, own, act, other, factor, penalty, sems):
    columns = pl.ds(pl.multiple_of((1 - core[0]) * HALF, HALF), HALF)
    copies = []
    for i in range(4):
        span = slice(128 * i, 128 * i + 128)
        copies.append(
            pltpu.make_async_copy(weight.at[span, columns], other.at[span, :], sems.at[i])
        )
        copies[-1].start()
    squares = jnp.zeros((TOKENS, 128), f32)
    for part in (own, other):
        if part is other:
            for copy in copies:
                copy.wait()
        for j in range(HALF // 128):
            wide = part[:, 128 * j : 128 * j + 128].astype(f32)
            squares = squares + wide * wide
    norms = jnp.sqrt(jnp.sum(squares, axis=1, keepdims=True) + norm_epsilon)
    act_sum = jnp.sum(act[...].astype(f32), axis=1, keepdims=True)
    factor[...] = sparsity_weight / TOKENS * (act_sum / norms)
    norms = jnp.broadcast_to(sparsity_weight * norms / TOKENS, (TOKENS, 128))
    penalty[...] = norms.T[:1, :]


def decoder_rows(core, after, weight, own, act):
    ins = [(core, pltpu.SMEM), (after, None), (weight, None), (own, VMEM), (act, VMEM)]
    outs = [((TOKENS, HALF), bf16, VMEM)]
    outs += [((TOKENS, 1), f32, VMEM), ((1, TOKENS), f32, VMEM)]
    scratch = [pltpu.SemaphoreType.DMA((4,))]
    return call(rows_kernel, outs, ins, scratch, 8, 0, 6 * 2**20)


def times_rows(a, b):
    return lax.dot_general(a, b, (((1,), (1,)), ((), ())), preferred_element_type=f32)


def join(pieces, out):
    for i, piece in enumerate(pieces):
        out[128 * i : 128 * i + 128, :] = piece[...]


def decoder_part(half, out, errors, weight, act, factor, stage, sems):
    copies = []
    for j in range(HALF // STEP):
        span = slice(j * STEP, j * STEP + STEP)
        part = jnp.dot(act[...], errors[:, span], preferred_element_type=f32)
        part = part + factor[...] * weight[:, span].astype(f32)
        stage[j] = part.astype(bf16)
        columns = pl.ds(pl.multiple_of(half * HALF + j * STEP, STEP), STEP)
        copies.append(pltpu.make_async_copy(stage.at[j], out.at[:, columns], sems.at[j]))
        copies[-1].start()
    return copies


def first_kernel(core, *refs):
    pieces, (weight, act, factor, grad_acts, out, errors, stage, sems) = refs[:4], refs[4:]
    join(pieces, errors)
    copies = decoder_part(core[0], out, errors, weight, act, factor, stage, sems)
    total = jnp.zeros((TOKENS, TOKENS), f32)
    for j in range(HALF // STEP):
        span = slice(j * STEP, j * STEP + STEP)
        total = total + times_rows(errors[:, span], weight[:, span])
    grad_acts[...] = total
    for copy in copies:
        copy.wait()


def first_gradients(core, errors, weight, act, factor):
    ins = [(core, pltpu.SMEM)] + [(v, VMEM) for v in [*errors, weight, act, factor]]
    outs = [((TOKENS, TOKENS), f32, VMEM), ((TOKENS, D), bf16, None)]
    scratch = [
        pltpu.VMEM((TOKENS, HALF), bf16),
        pltpu.VMEM((HALF // STEP, TOKENS, STEP), bf16),
        pltpu.SemaphoreType.DMA((HALF // STEP,)),
    ]
    flops = 4 * TOKENS * TOKENS * HALF
    return call(first_kernel, outs, ins, scratch, 24, flops, 8 * 2**20)


def last_kernel(core, _, own_acts, *refs):
    pieces, refs = refs[:4], refs[4:]
    (weight, act, factor, penalty, rectified, flipped_own, flipped_mate) = refs[:7]
    (out, out_encoder, out_bias) = refs[7:10]
    (errors, stage, turned, grads, grads_mate, encoder_stage, sems, encoder_sems) = refs[10:]
    join(pieces, errors)
    turned[...] = times_rows(errors[...], weight[...])
    bias = jnp.zeros((1, TOKENS), f32)
    for major in range(4):
        for minor in range(4):
            here, there = (major * 4 + minor) * 32, (minor * 4 + major) * 32
            acts = own_acts[here : here + 32, :] + turned[there : there + 32, :] + penalty[...]
            rounded = (acts * 2.0 * rectified[here : here + 32, :]).astype(bf16)
            grads[here : here + 32, :] = rounded
            grads_mate[there : there + 32, :] = rounded
            bias = bias + jnp.sum(rounded.astype(f32), axis=0, keepdims=True)
    out_bias[...] = bias
    copies = []
    for k, (flipped, grad) in enumerate(((flipped_own, grads), (flipped_mate, grads_mate))):
        half = core[0] if k == 0 else 1 - core[0]
        for j in range(HALF // STEP):
            slot = k * (HALF // STEP) + j
            part = flipped[j * STEP : j * STEP + STEP, :]
            part = jnp.dot(part, grad[...], preferred_element_type=f32)
            encoder_stage[slot] = part.astype(bf16)
            rows = pl.ds(pl.multiple_of(half * HALF + j * STEP, STEP), STEP)
            copies.append(
                pltpu.make_async_copy(
                    encoder_stage.at[slot], out_encoder.at[rows, :], encoder_sems.at[slot]
                )
            )
            copies[-1].start()
    copies += decoder_part(1 - core[0], out, errors, weight, act, factor, stage, sems)
    for copy in copies:
        copy.wait()


def last_gradients(core, grad_decoder, grad_acts, errors, *rest):
    ins = [(core, pltpu.SMEM), (grad_decoder, None), (grad_acts, VMEM)]
    ins += [(v, VMEM) for v in [*errors, *rest]]
    outs = [((TOKENS, D), bf16, None), ((D, TOKENS), bf16, None), ((1, TOKENS), f32, VMEM)]
    steps = HALF // STEP
    scratch = [
        pltpu.VMEM((TOKENS, HALF), bf16),
        pltpu.VMEM((steps, TOKENS, STEP), bf16),
        pltpu.VMEM((TOKENS, TOKENS), f32),
        pltpu.VMEM((TOKENS, TOKENS), bf16),
        pltpu.VMEM((TOKENS, TOKENS), bf16),
        pltpu.VMEM((2 * steps, STEP, TOKENS), bf16),
        pltpu.SemaphoreType.DMA((steps,)),
        pltpu.SemaphoreType.DMA((2 * steps,)),
    ]
    flops = 8 * TOKENS * TOKENS * HALF
    return call(
        last_kernel, outs, ins, scratch, 32, flops, 16 * 2**20, input_output_aliases={1: 0}
    )


def dot(a, b):
    return jnp.dot(a, b, preferred_element_type=f32)


def local(
    head_outputs,
    out_weight,
    residual_input,
    post_gain,
    encoder_weight,
    encoder_bias,
    decoder_weight,
    decoder_bias,
):
    here = lax.axis_index("prod")
    low = here // 2 == 0
    first = here % 2 == 0

    def own_half(v):
        return jnp.where(first, v[..., :HALF], v[..., HALF:])

    def other_half(v):
        return jnp.where(first, v[..., HALF:], v[..., :HALF])

    core = (here % 2).reshape(1)
    partial_value = dot(head_outputs, out_weight)
    both = own_half(partial_value) + to_core(other_half(partial_value))
    encoder_other = cut(encoder_weight, 0, 1 - core, both)
    decoder_other = cut(decoder_weight, 1, 1 - core, both)
    projected = both + lax.ppermute(both, "prod", [(0, 2), (2, 0), (1, 3), (3, 1)])
    projected, encoder_other, decoder_other = lax.optimization_barrier(
        (projected, encoder_other, decoder_other)
    )
    squares = jnp.broadcast_to(jnp.sum(projected * projected, axis=1, keepdims=True), (16, 128))
    squares = (squares + to_core(squares))[:, :1]
    gain = own_half(post_gain)
    normed = projected * lax.rsqrt(squares / D + norm_epsilon) * gain
    stream = (own_half(residual_input).astype(f32) + normed).astype(bf16)
    stream = jnp.where(low, stream, jnp.roll(stream, 8, axis=0))

    stream, encoder_other, decoder_other = lax.optimization_barrier(
        (stream, encoder_other, decoder_other)
    )
    encoder_mate = to_core(encoder_other)
    decoder_mate = to_core(decoder_other)
    bias_own = own_half(decoder_bias)
    stream = jnp.concatenate([stream, to_y(stream, 3)])
    stream = jnp.concatenate([stream] + [to_minor(stream, -d) for d in (1, 2, 3)])
    own_stream = stream.reshape(4, 4, 8, HALF)[:, 0].reshape(32, HALF)
    centred = (stream.astype(f32) - bias_own).astype(bf16)
    centred, encoder_mate, decoder_mate = lax.optimization_barrier(
        (centred, encoder_mate, decoder_mate)
    )
    encoder_mate = cut(encoder_mate, 0, core * 0, centred)
    decoder_mate = cut(decoder_mate, 1, core * 0, centred)
    encoder_own = cut(encoder_weight, 0, core, centred)
    decoder_own = cut(decoder_weight, 1, core, centred)
    centred = [centred] + [to_major(centred, -d) for d in (1, 2, 3)]

    for_mate = swap_blocks(jnp.concatenate([dot(piece, encoder_mate) for piece in centred]))
    for_mate, decoder_own, decoder_mate = lax.optimization_barrier(
        (for_mate, decoder_own, decoder_mate)
    )
    preact = jnp.concatenate([dot(piece, encoder_own) for piece in centred])
    preact = preact + to_core(for_mate) + encoder_bias
    rectified = jnp.maximum(preact, 0.0)
    activations = jnp.square(rectified).astype(bf16)
    swapped = swap_blocks(activations)
    mate_activations = to_core(swapped)

    own = product(activations, decoder_own)
    pieces = {}
    for d in range(4):
        rows = slice(128 * d, 128 * d + 128)
        pieces[d] = (own[rows] + dot(mate_activations[rows], decoder_mate)).astype(bf16)
    far = pieces[2].reshape(4, 4, 8, HALF)
    keep = jnp.where(first, far[:, :2], far[:, ::2])
    send = jnp.where(first, far[:, 2:], far[:, 1::2])
    send = move(send, lambda x, y, z, c: (x, y ^ (3 if c == 0 else 1), z, c))
    far = (keep.astype(f32) + send.astype(f32)).astype(bf16)
    send = move(far[:, 1], lambda x, y, z, c: (x, y ^ (1 if c == 0 else 3), z, c))
    far = (far[:, 0].astype(f32) + send.astype(f32)).astype(bf16).reshape(32, HALF)
    recon = [pieces[0], to_major(pieces[1], 1), to_major(pieces[3], 3)]
    recon = sum(piece.astype(f32) for piece in recon).astype(bf16)
    flipped_own, flipped_act, flipped_swapped = flip(centred, [activations, swapped], pieces[0])
    decoder_other, factor, penalty = decoder_rows(
        core, pieces[0], decoder_weight, decoder_own, flipped_act
    )
    recon, flipped_own, decoder_other, factor, penalty = lax.optimization_barrier(
        (recon, flipped_own, decoder_other, factor, penalty)
    )
    flipped_mate = to_core(flipped_own)
    recon = (scatter_y(recon) + to_major(far, 2).astype(f32)).astype(bf16)
    summed = recon.astype(f32)
    for d in (1, 2, 3):
        summed = summed + jnp.roll(to_minor(recon, -d), 8 * d, axis=0).astype(f32)
    grad_recon = (2.0 * (summed + bias_own - own_stream.astype(f32)) / TOKENS).astype(bf16)

    far = to_major(grad_recon, 2)
    errors = gather_y(grad_recon)
    errors, flipped_mate = lax.optimization_barrier((errors, flipped_mate))
    errors = [errors, to_major(errors, -1), gather_y(far), to_major(errors, -3)]
    errors_mate = [to_core(piece) for piece in errors]

    grad_acts, grad_decoder = first_gradients(core, errors, decoder_own, flipped_act, factor)
    grad_decoder, grad_encoder, grad_bias = last_gradients(
        core, grad_decoder, grad_acts, errors_mate, decoder_other, flipped_swapped, factor,
        penalty, rectified, flipped_own, flipped_mate,
    )
    return (grad_encoder, grad_bias.reshape(TOKENS), grad_decoder)


def solution(mesh):
    placed = (
        P("sae", "prod"),
        P("prod", None),
        P("sae", None),
        P(),
        P(None, ("prod", "sae")),
        P(("prod", "sae")),
        P(("prod", "sae"), None),
        P(),
    )
    return jax.shard_map(
        local,
        mesh=mesh,
        in_specs=placed,
        out_specs=(P(None, ("prod", "sae")), P(("prod", "sae")), P(("prod", "sae"), None)),
        check_vma=False,
    )
```

```python
import functools

import jax
import jax.numpy as jnp
from jax import lax
from jax.experimental import pallas as pl
from jax.experimental.pallas import tpu as pltpu
from jax.sharding import PartitionSpec as P

sparsity_weight = 4.0
norm_epsilon = 1e-06
TOKENS = 512
D = 4608
HALF = D // 2
AXES = ("prod", "sae")
STEP = 768
VMEM = pltpu.VMEM
bf16 = jnp.bfloat16
f32 = jnp.float32


def place(x, y, z, c):
    return ((y % 2) * 2 + c) * 32 + (x * 4 + z) * 2 + y // 2


def route(step):
    pairs = []
    for x in range(4):
        for y in range(4):
            for z in range(4):
                for c in range(2):
                    tx, ty, tz, tc = step(x, y, z, c)
                    pairs.append((place(x, y, z, c), place(tx % 4, ty % 4, tz % 4, tc % 2)))
    return pairs


def move(value, step):
    return lax.ppermute(value, AXES, route(step))


def to_core(value):
    return move(value, lambda x, y, z, c: (x, y, z, 1 - c))


def to_major(value, d):
    return move(value, lambda x, y, z, c: (x + d, y, z, c) if c == 0 else (x, y, z + d, c))


def to_y(value, mask):
    return move(value, lambda x, y, z, c: (x, y ^ mask, z, c))


def to_minor(value, d):
    return move(value, lambda x, y, z, c: (x, y, z + d, c) if c == 0 else (x + d, y, z, c))


MASKS = (0, 1, 3, 2)


def gather_y(value):
    pieces = [value] + [to_y(value, mask) for mask in MASKS[1:]]
    pieces = [piece.reshape(4, 1, 8, HALF) for piece in pieces]
    return jnp.concatenate(pieces, axis=1).reshape(128, HALF)


def scatter_y(value):
    pieces = [value.reshape(4, 4, 8, HALF)[:, k].reshape(32, HALF) for k in range(4)]
    pieces = pieces[:1] + [to_y(piece, mask) for piece, mask in zip(pieces[1:], MASKS[1:])]
    return sum(piece.astype(f32) for piece in pieces)


def swap_blocks(value):
    return value.reshape(4, 4, 32, value.shape[-1]).transpose(1, 0, 2, 3).reshape(value.shape)


def product_kernel(a, b, out):
    for j in range(HALF // STEP):
        span = slice(j * STEP, j * STEP + STEP)
        out[:, span] = jnp.dot(a[...], b[:, span], preferred_element_type=f32)


def product(a, b):
    outs = [((a.shape[0], b.shape[1]), f32, VMEM)]
    return call(product_kernel, outs, [(a, VMEM), (b, VMEM)], [], 12, 1024, 1024)[0]


def cut_kernel(axis, half_ref, after_ref, weight_ref, out_ref, sems):
    start, rows = half_ref[0] * HALF, out_ref.shape[0] // 4
    copies = []
    for i in range(4):
        if axis == 0:
            part = weight_ref.at[pl.ds(pl.multiple_of(start + i * rows, rows), rows), :]
        else:
            part = weight_ref.at[pl.ds(i * rows, rows), pl.ds(pl.multiple_of(start, HALF), HALF)]
        out = out_ref.at[pl.ds(i * rows, rows), :]
        copies.append(pltpu.make_async_copy(part, out, sems.at[i]))
        copies[-1].start()
    for copy in copies:
        copy.wait()


def cut(weight, axis, half, after):
    shape = (HALF, weight.shape[1]) if axis == 0 else (weight.shape[0], HALF)
    ins = [(half, pltpu.SMEM), (after, None), (weight, None)]
    kernel = functools.partial(cut_kernel, axis)
    scratch = [pltpu.SemaphoreType.DMA((4,))]
    return call(kernel, [(shape, bf16, VMEM)], ins, scratch, 4, 0, weight.size * 2)[0]


def call(kernel, outs, ins, scratch, mib, flops, data, **more):
    def spec(space):
        return pl.BlockSpec(memory_space=pl.ANY if space is None else space)

    return pl.pallas_call(
        kernel,
        out_shape=tuple(jax.ShapeDtypeStruct(shape, dtype) for shape, dtype, _ in outs),
        in_specs=[spec(space) for _, space in ins],
        out_specs=tuple(spec(space) for *_, space in outs),
        scratch_shapes=scratch,
        compiler_params=pltpu.CompilerParams(vmem_limit_bytes=mib * 2**20),
        cost_estimate=pl.CostEstimate(flops=flops, bytes_accessed=data, transcendentals=0),
        **more,
    )(*(value for value, _ in ins))


def flip_kernel(*refs):
    pieces, squares, (norms, _, out, *square_outs, factor) = refs[:4], refs[4:6], refs[6:]
    for k, piece in enumerate(pieces):

        def tile(j, carry, piece=piece, column=128 * k):
            rows = pl.ds(pl.multiple_of(j * 256, 256), 256)
            out[rows, column : column + 128] = piece[:, rows].T
            return carry

        lax.fori_loop(0, HALF // 256, tile, 0)
    for square, square_out in zip(squares, square_outs):
        for i in range(4):
            square_out[:, 128 * i : 128 * i + 128] = square[128 * i : 128 * i + 128, :].T
    act_sum = jnp.sum(square_outs[0][...].astype(f32), axis=1, keepdims=True)
    factor[...] = sparsity_weight / TOKENS * (act_sum / norms[...])


def flip(pieces, squares, norms, after):
    ins = [(v, VMEM) for v in pieces + squares + [norms]] + [(after, None)]
    outs = [((HALF, TOKENS), bf16, VMEM)] + [((TOKENS, TOKENS), bf16, VMEM)] * 2
    outs += [((TOKENS, 1), f32, VMEM)]
    return call(flip_kernel, outs, ins, [], 8, 0, 6 * 2**20)


def rows_kernel(core, _, weight, own, other, norms_out, penalty, sems):
    columns = pl.ds(pl.multiple_of((1 - core[0]) * HALF, HALF), HALF)
    copies = []
    for i in range(4):
        span = slice(128 * i, 128 * i + 128)
        copies.append(
            pltpu.make_async_copy(weight.at[span, columns], other.at[span, :], sems.at[i])
        )
        copies[-1].start()
    squares = jnp.zeros((TOKENS, 128), f32)
    for part in (own, other):
        if part is other:
            for copy in copies:
                copy.wait()
        for j in range(HALF // 128):
            wide = part[:, 128 * j : 128 * j + 128].astype(f32)
            squares = squares + wide * wide
    norms = jnp.sqrt(jnp.sum(squares, axis=1, keepdims=True) + norm_epsilon)
    norms_out[...] = norms
    norms = jnp.broadcast_to(sparsity_weight * norms / TOKENS, (TOKENS, 128))
    penalty[...] = norms.T[:1, :]


def decoder_rows(core, after, weight, own):
    ins = [(core, pltpu.SMEM), (after, None), (weight, None), (own, VMEM)]
    outs = [((TOKENS, HALF), bf16, VMEM)]
    outs += [((TOKENS, 1), f32, VMEM), ((1, TOKENS), f32, VMEM)]
    scratch = [pltpu.SemaphoreType.DMA((4,))]
    return call(rows_kernel, outs, ins, scratch, 8, 0, 6 * 2**20)


def times_rows(a, b):
    return lax.dot_general(a, b, (((1,), (1,)), ((), ())), preferred_element_type=f32)


def join(pieces, out):
    for i, piece in enumerate(pieces):
        out[128 * i : 128 * i + 128, :] = piece[...]


def decoder_part(half, out, errors, weight, act, factor, stage, sems):
    step = stage.shape[-1]
    copies = []
    for j in range(HALF // step):
        span = slice(j * step, j * step + step)
        part = jnp.dot(act[...], errors[:, span], preferred_element_type=f32)
        part = part + factor[...] * weight[:, span].astype(f32)
        stage[j] = part.astype(bf16)
        columns = pl.ds(pl.multiple_of(half * HALF + j * step, step), step)
        copies.append(pltpu.make_async_copy(stage.at[j], out.at[:, columns], sems.at[j]))
        copies[-1].start()
    return copies


def first_kernel(core, *refs):
    pieces, (weight, act, factor, grad_acts, out, errors, stage, sems) = refs[:4], refs[4:]
    join(pieces, errors)
    copies = decoder_part(core[0], out, errors, weight, act, factor, stage, sems)
    grad_acts[...] = times_rows(errors[...], weight[...])
    for copy in copies:
        copy.wait()


def first_gradients(core, errors, weight, act, factor):
    ins = [(core, pltpu.SMEM)] + [(v, VMEM) for v in [*errors, weight, act, factor]]
    outs = [((TOKENS, TOKENS), f32, VMEM), ((TOKENS, D), bf16, None)]
    scratch = [
        pltpu.VMEM((TOKENS, HALF), bf16),
        pltpu.VMEM((2, TOKENS, HALF // 2), bf16),
        pltpu.SemaphoreType.DMA((2,)),
    ]
    flops = 4 * TOKENS * TOKENS * HALF
    return call(first_kernel, outs, ins, scratch, 24, flops, 8 * 2**20)


def last_kernel(core, _, own_acts, *refs):
    pieces, refs = refs[:4], refs[4:]
    (weight, act, factor, penalty, rectified, flipped_own, flipped_mate) = refs[:7]
    (out, out_encoder, out_bias) = refs[7:10]
    (errors, stage, turned, grads, grads_mate, encoder_stage, sems, encoder_sems) = refs[10:]
    join(pieces, errors)
    turned[...] = times_rows(errors[...], weight[...])
    bias = jnp.zeros((1, TOKENS), f32)
    for major in range(4):
        for minor in range(4):
            here, there = (major * 4 + minor) * 32, (minor * 4 + major) * 32
            acts = own_acts[here : here + 32, :] + turned[there : there + 32, :] + penalty[...]
            rounded = (acts * 2.0 * rectified[here : here + 32, :]).astype(bf16)
            grads[here : here + 32, :] = rounded
            grads_mate[there : there + 32, :] = rounded
            bias = bias + jnp.sum(rounded.astype(f32), axis=0, keepdims=True)
    out_bias[...] = bias
    copies = []
    for k, (flipped, grad) in enumerate(((flipped_own, grads), (flipped_mate, grads_mate))):
        half = core[0] if k == 0 else 1 - core[0]
        for j in range(HALF // STEP):
            slot = k * (HALF // STEP) + j
            part = flipped[j * STEP : j * STEP + STEP, :]
            part = jnp.dot(part, grad[...], preferred_element_type=f32)
            encoder_stage[slot] = part.astype(bf16)
            rows = pl.ds(pl.multiple_of(half * HALF + j * STEP, STEP), STEP)
            copies.append(
                pltpu.make_async_copy(
                    encoder_stage.at[slot], out_encoder.at[rows, :], encoder_sems.at[slot]
                )
            )
            copies[-1].start()
    copies += decoder_part(1 - core[0], out, errors, weight, act, factor, stage, sems)
    for copy in copies:
        copy.wait()


def last_gradients(core, grad_decoder, grad_acts, errors, *rest):
    ins = [(core, pltpu.SMEM), (grad_decoder, None), (grad_acts, VMEM)]
    ins += [(v, VMEM) for v in [*errors, *rest]]
    outs = [((TOKENS, D), bf16, None), ((D, TOKENS), bf16, None), ((1, TOKENS), f32, VMEM)]
    steps = HALF // STEP
    scratch = [
        pltpu.VMEM((TOKENS, HALF), bf16),
        pltpu.VMEM((steps, TOKENS, STEP), bf16),
        pltpu.VMEM((TOKENS, TOKENS), f32),
        pltpu.VMEM((TOKENS, TOKENS), bf16),
        pltpu.VMEM((TOKENS, TOKENS), bf16),
        pltpu.VMEM((2 * steps, STEP, TOKENS), bf16),
        pltpu.SemaphoreType.DMA((steps,)),
        pltpu.SemaphoreType.DMA((2 * steps,)),
    ]
    flops = 8 * TOKENS * TOKENS * HALF
    return call(
        last_kernel, outs, ins, scratch, 32, flops, 16 * 2**20, input_output_aliases={1: 0}
    )


def dot(a, b):
    return jnp.dot(a, b, preferred_element_type=f32)


def local(
    head_outputs,
    out_weight,
    residual_input,
    post_gain,
    encoder_weight,
    encoder_bias,
    decoder_weight,
    decoder_bias,
):
    here = lax.axis_index("prod")
    low = here // 2 == 0
    first = here % 2 == 0

    def own_half(v):
        return jnp.where(first, v[..., :HALF], v[..., HALF:])

    def other_half(v):
        return jnp.where(first, v[..., HALF:], v[..., :HALF])

    core = (here % 2).reshape(1)
    partial_value = dot(head_outputs, out_weight)
    both = own_half(partial_value) + to_core(other_half(partial_value))
    encoder_other = cut(encoder_weight, 0, 1 - core, both)
    decoder_other = cut(decoder_weight, 1, 1 - core, both)
    projected = both + lax.ppermute(both, "prod", [(0, 2), (2, 0), (1, 3), (3, 1)])
    projected, encoder_other, decoder_other = lax.optimization_barrier(
        (projected, encoder_other, decoder_other)
    )
    squares = jnp.broadcast_to(jnp.sum(projected * projected, axis=1, keepdims=True), (16, 128))
    squares = (squares + to_core(squares))[:, :1]
    gain = own_half(post_gain)
    normed = projected * lax.rsqrt(squares / D + norm_epsilon) * gain
    stream = (own_half(residual_input).astype(f32) + normed).astype(bf16)
    stream = jnp.where(low, stream, jnp.roll(stream, 8, axis=0))

    stream, encoder_other, decoder_other = lax.optimization_barrier(
        (stream, encoder_other, decoder_other)
    )
    encoder_mate = to_core(encoder_other)
    decoder_mate = to_core(decoder_other)
    bias_own = own_half(decoder_bias)
    stream = jnp.concatenate([stream, to_y(stream, 3)])
    stream = jnp.concatenate([stream] + [to_minor(stream, -d) for d in (1, 2, 3)])
    own_stream = stream.reshape(4, 4, 8, HALF)[:, 0].reshape(32, HALF)
    centred = (stream.astype(f32) - bias_own).astype(bf16)
    centred, encoder_mate, decoder_mate = lax.optimization_barrier(
        (centred, encoder_mate, decoder_mate)
    )
    encoder_mate = cut(encoder_mate, 0, core * 0, centred)
    decoder_mate = cut(decoder_mate, 1, core * 0, centred)
    encoder_own = cut(encoder_weight, 0, core, centred)
    decoder_own = cut(decoder_weight, 1, core, centred)
    centred = [centred] + [to_major(centred, -d) for d in (1, 2, 3)]

    for_mate = swap_blocks(jnp.concatenate([dot(piece, encoder_mate) for piece in centred]))
    decoder_other, norms, penalty = decoder_rows(core, centred[0], decoder_weight, decoder_own)
    for_mate, decoder_own, decoder_mate, decoder_other, norms, penalty = lax.optimization_barrier(
        (for_mate, decoder_own, decoder_mate, decoder_other, norms, penalty)
    )
    preact = jnp.concatenate([dot(piece, encoder_own) for piece in centred])
    preact = preact + to_core(for_mate) + encoder_bias
    rectified = jnp.maximum(preact, 0.0)
    activations = jnp.square(rectified).astype(bf16)
    swapped = swap_blocks(activations)
    mate_activations = to_core(swapped)

    own = product(activations, decoder_own)
    pieces = {}
    for d in range(4):
        rows = slice(128 * d, 128 * d + 128)
        pieces[d] = (own[rows] + dot(mate_activations[rows], decoder_mate)).astype(bf16)
    far = pieces[2].reshape(4, 4, 8, HALF)
    keep = jnp.where(first, far[:, :2], far[:, ::2])
    send = jnp.where(first, far[:, 2:], far[:, 1::2])
    send = move(send, lambda x, y, z, c: (x, y ^ (3 if c == 0 else 1), z, c))
    far = (keep.astype(f32) + send.astype(f32)).astype(bf16)
    send = move(far[:, 1], lambda x, y, z, c: (x, y ^ (1 if c == 0 else 3), z, c))
    far = (far[:, 0].astype(f32) + send.astype(f32)).astype(bf16).reshape(32, HALF)
    recon = [pieces[0], to_major(pieces[1], 1), to_major(pieces[3], 3)]
    recon = sum(piece.astype(f32) for piece in recon).astype(bf16)
    flipped_own, flipped_act, flipped_swapped, factor = flip(
        centred, [activations, swapped], norms, pieces[0]
    )
    recon, flipped_own = lax.optimization_barrier((recon, flipped_own))
    flipped_mate = to_core(flipped_own)
    recon = (scatter_y(recon) + to_major(far, 2).astype(f32)).astype(bf16)
    summed = recon.astype(f32)
    for d in (1, 2, 3):
        summed = summed + jnp.roll(to_minor(recon, -d), 8 * d, axis=0).astype(f32)
    grad_recon = (2.0 * (summed + bias_own - own_stream.astype(f32)) / TOKENS).astype(bf16)

    far = to_major(grad_recon, 2)
    errors = gather_y(grad_recon)
    errors, flipped_mate = lax.optimization_barrier((errors, flipped_mate))
    errors = [errors, to_major(errors, -1), gather_y(far), to_major(errors, -3)]
    errors_mate = [to_core(piece) for piece in errors]

    grad_acts, grad_decoder = first_gradients(core, errors, decoder_own, flipped_act, factor)
    grad_decoder, grad_encoder, grad_bias = last_gradients(
        core, grad_decoder, grad_acts, errors_mate, decoder_other, flipped_swapped, factor,
        penalty, rectified, flipped_own, flipped_mate,
    )
    return (grad_encoder, grad_bias.reshape(TOKENS), grad_decoder)


def solution(mesh):
    placed = (
        P("sae", "prod"),
        P("prod", None),
        P("sae", None),
        P(),
        P(None, ("prod", "sae")),
        P(("prod", "sae")),
        P(("prod", "sae"), None),
        P(),
    )
    return jax.shard_map(
        local,
        mesh=mesh,
        in_specs=placed,
        out_specs=(P(None, ("prod", "sae")), P(("prod", "sae")), P(("prod", "sae"), None)),
        check_vma=False,
    )
```

```python
import functools

import jax
import jax.numpy as jnp
from jax import lax
from jax.experimental import pallas as pl
from jax.experimental.pallas import tpu as pltpu
from jax.sharding import PartitionSpec as P

sparsity_weight = 4.0
norm_epsilon = 1e-06
TOKENS = 512
D = 4608
HALF = D // 2
AXES = ("prod", "sae")
STEP = 768
VMEM = pltpu.VMEM
bf16 = jnp.bfloat16
f32 = jnp.float32


def place(x, y, z, c):
    return ((y % 2) * 2 + c) * 32 + (x * 4 + z) * 2 + y // 2


def route(step):
    pairs = []
    for x in range(4):
        for y in range(4):
            for z in range(4):
                for c in range(2):
                    tx, ty, tz, tc = step(x, y, z, c)
                    pairs.append((place(x, y, z, c), place(tx % 4, ty % 4, tz % 4, tc % 2)))
    return pairs


def move(value, step):
    return lax.ppermute(value, AXES, route(step))


def to_core(value):
    return move(value, lambda x, y, z, c: (x, y, z, 1 - c))


def to_major(value, d):
    return move(value, lambda x, y, z, c: (x + d, y, z, c) if c == 0 else (x, y, z + d, c))


def to_y(value, mask):
    return move(value, lambda x, y, z, c: (x, y ^ mask, z, c))


def to_minor(value, d):
    return move(value, lambda x, y, z, c: (x, y, z + d, c) if c == 0 else (x + d, y, z, c))


MASKS = (0, 1, 3, 2)


def gather_y(value):
    pieces = [value] + [to_y(value, mask) for mask in MASKS[1:]]
    pieces = [piece.reshape(4, 1, 8, HALF) for piece in pieces]
    return jnp.concatenate(pieces, axis=1).reshape(128, HALF)


def scatter_y(value):
    pieces = [value.reshape(4, 4, 8, HALF)[:, k].reshape(32, HALF) for k in range(4)]
    pieces = pieces[:1] + [to_y(piece, mask) for piece, mask in zip(pieces[1:], MASKS[1:])]
    return sum(piece.astype(f32) for piece in pieces)


def swap_blocks(value):
    return value.reshape(4, 4, 32, value.shape[-1]).transpose(1, 0, 2, 3).reshape(value.shape)


def product_kernel(a, b, out):
    for j in range(HALF // STEP):
        span = slice(j * STEP, j * STEP + STEP)
        out[:, span] = jnp.dot(a[...], b[:, span], preferred_element_type=f32)


def product(a, b):
    outs = [((a.shape[0], b.shape[1]), f32, VMEM)]
    return call(product_kernel, outs, [(a, VMEM), (b, VMEM)], [], 12, 1024, 1024)[0]


def cut_kernel(axis, half_ref, after_ref, weight_ref, out_ref, sems):
    start, rows = half_ref[0] * HALF, out_ref.shape[0] // 4
    copies = []
    for i in range(4):
        if axis == 0:
            part = weight_ref.at[pl.ds(pl.multiple_of(start + i * rows, rows), rows), :]
        else:
            part = weight_ref.at[pl.ds(i * rows, rows), pl.ds(pl.multiple_of(start, HALF), HALF)]
        out = out_ref.at[pl.ds(i * rows, rows), :]
        copies.append(pltpu.make_async_copy(part, out, sems.at[i]))
        copies[-1].start()
    for copy in copies:
        copy.wait()


def cut(weight, axis, half, after):
    shape = (HALF, weight.shape[1]) if axis == 0 else (weight.shape[0], HALF)
    ins = [(half, pltpu.SMEM), (after, None), (weight, None)]
    kernel = functools.partial(cut_kernel, axis)
    scratch = [pltpu.SemaphoreType.DMA((4,))]
    return call(kernel, [(shape, bf16, VMEM)], ins, scratch, 4, 0, weight.size * 2)[0]


def call(kernel, outs, ins, scratch, mib, flops, data, **more):
    def spec(space):
        return pl.BlockSpec(memory_space=pl.ANY if space is None else space)

    return pl.pallas_call(
        kernel,
        out_shape=tuple(jax.ShapeDtypeStruct(shape, dtype) for shape, dtype, _ in outs),
        in_specs=[spec(space) for _, space in ins],
        out_specs=tuple(spec(space) for *_, space in outs),
        scratch_shapes=scratch,
        compiler_params=pltpu.CompilerParams(vmem_limit_bytes=mib * 2**20),
        cost_estimate=pl.CostEstimate(flops=flops, bytes_accessed=data, transcendentals=0),
        **more,
    )(*(value for value, _ in ins))


def flip_kernel(*refs):
    pieces, squares, (norms, _, out, *square_outs, factor) = refs[:4], refs[4:6], refs[6:]
    for k, piece in enumerate(pieces):

        def tile(j, carry, piece=piece, column=128 * k):
            rows = pl.ds(pl.multiple_of(j * 256, 256), 256)
            out[rows, column : column + 128] = piece[:, rows].T
            return carry

        lax.fori_loop(0, HALF // 256, tile, 0)
    for square, square_out in zip(squares, square_outs):
        for i in range(4):
            square_out[:, 128 * i : 128 * i + 128] = square[128 * i : 128 * i + 128, :].T
    act_sum = jnp.sum(square_outs[0][...].astype(f32), axis=1, keepdims=True)
    factor[...] = sparsity_weight / TOKENS * (act_sum / norms[...])


def flip(pieces, squares, norms, after):
    ins = [(v, VMEM) for v in pieces + squares + [norms]] + [(after, None)]
    outs = [((HALF, TOKENS), bf16, VMEM)] + [((TOKENS, TOKENS), bf16, VMEM)] * 2
    outs += [((TOKENS, 1), f32, VMEM)]
    return call(flip_kernel, outs, ins, [], 8, 0, 6 * 2**20)


def rows_kernel(core, _, weight, own, other, norms_out, penalty, sems):
    columns = pl.ds(pl.multiple_of((1 - core[0]) * HALF, HALF), HALF)
    copies = []
    for i in range(4):
        span = slice(128 * i, 128 * i + 128)
        copies.append(
            pltpu.make_async_copy(weight.at[span, columns], other.at[span, :], sems.at[i])
        )
        copies[-1].start()
    squares = jnp.zeros((TOKENS, 128), f32)
    for part in (own, other):
        if part is other:
            for copy in copies:
                copy.wait()
        for j in range(HALF // 128):
            wide = part[:, 128 * j : 128 * j + 128].astype(f32)
            squares = squares + wide * wide
    norms = jnp.sqrt(jnp.sum(squares, axis=1, keepdims=True) + norm_epsilon)
    norms_out[...] = norms
    norms = jnp.broadcast_to(sparsity_weight * norms / TOKENS, (TOKENS, 128))
    penalty[...] = norms.T[:1, :]


def decoder_rows(core, after, weight, own):
    ins = [(core, pltpu.SMEM), (after, None), (weight, None), (own, VMEM)]
    outs = [((TOKENS, HALF), bf16, VMEM)]
    outs += [((TOKENS, 1), f32, VMEM), ((1, TOKENS), f32, VMEM)]
    scratch = [pltpu.SemaphoreType.DMA((4,))]
    return call(rows_kernel, outs, ins, scratch, 8, 0, 6 * 2**20)


def times_rows(a, b):
    return lax.dot_general(a, b, (((1,), (1,)), ((), ())), preferred_element_type=f32)


def join(pieces, out):
    for i, piece in enumerate(pieces):
        out[128 * i : 128 * i + 128, :] = piece[...]


def decoder_part(half, out, errors, weight, act, factor, stage, sems):
    step = stage.shape[-1]
    copies = []
    for j in range(HALF // step):
        span = slice(j * step, j * step + step)
        part = jnp.dot(act[...], errors[:, span], preferred_element_type=f32)
        part = part + factor[...] * weight[:, span].astype(f32)
        stage[j] = part.astype(bf16)
        columns = pl.ds(pl.multiple_of(half * HALF + j * step, step), step)
        copies.append(pltpu.make_async_copy(stage.at[j], out.at[:, columns], sems.at[j]))
        copies[-1].start()
    return copies


def first_kernel(core, *refs):
    pieces, (weight, act, factor, grad_acts, out, errors, stage, sems) = refs[:4], refs[4:]
    join(pieces, errors)
    copies = decoder_part(core[0], out, errors, weight, act, factor, stage, sems)
    grad_acts[...] = times_rows(errors[...], weight[...])
    for copy in copies:
        copy.wait()


def first_gradients(core, errors, weight, act, factor):
    ins = [(core, pltpu.SMEM)] + [(v, VMEM) for v in [*errors, weight, act, factor]]
    outs = [((TOKENS, TOKENS), f32, VMEM), ((TOKENS, D), bf16, None)]
    scratch = [
        pltpu.VMEM((TOKENS, HALF), bf16),
        pltpu.VMEM((2, TOKENS, HALF // 2), bf16),
        pltpu.SemaphoreType.DMA((2,)),
    ]
    flops = 4 * TOKENS * TOKENS * HALF
    return call(first_kernel, outs, ins, scratch, 24, flops, 8 * 2**20)


def last_kernel(core, _, own_acts, *refs):
    pieces, refs = refs[:4], refs[4:]
    (weight, act, factor, penalty, rectified, flipped_own, flipped_mate) = refs[:7]
    (out, out_encoder, out_bias) = refs[7:10]
    (errors, stage, turned, grads, grads_mate, encoder_stage, sems, encoder_sems) = refs[10:]
    join(pieces, errors)
    turned[...] = times_rows(errors[...], weight[...])
    bias = jnp.zeros((1, TOKENS), f32)
    for major in range(4):
        for minor in range(4):
            here, there = (major * 4 + minor) * 32, (minor * 4 + major) * 32
            acts = own_acts[here : here + 32, :] + turned[there : there + 32, :] + penalty[...]
            rounded = (acts * 2.0 * rectified[here : here + 32, :]).astype(bf16)
            grads[here : here + 32, :] = rounded
            grads_mate[there : there + 32, :] = rounded
            bias = bias + jnp.sum(rounded.astype(f32), axis=0, keepdims=True)
    out_bias[...] = bias
    copies = []
    for k, (flipped, grad) in enumerate(((flipped_own, grads), (flipped_mate, grads_mate))):
        half = core[0] if k == 0 else 1 - core[0]
        for j in range(HALF // STEP):
            slot = k * (HALF // STEP) + j
            part = flipped[j * STEP : j * STEP + STEP, :]
            part = jnp.dot(part, grad[...], preferred_element_type=f32)
            encoder_stage[slot] = part.astype(bf16)
            rows = pl.ds(pl.multiple_of(half * HALF + j * STEP, STEP), STEP)
            copies.append(
                pltpu.make_async_copy(
                    encoder_stage.at[slot], out_encoder.at[rows, :], encoder_sems.at[slot]
                )
            )
            copies[-1].start()
    copies += decoder_part(1 - core[0], out, errors, weight, act, factor, stage, sems)
    for copy in copies:
        copy.wait()


def last_gradients(core, grad_decoder, grad_acts, errors, *rest):
    ins = [(core, pltpu.SMEM), (grad_decoder, None), (grad_acts, VMEM)]
    ins += [(v, VMEM) for v in [*errors, *rest]]
    outs = [((TOKENS, D), bf16, None), ((D, TOKENS), bf16, None), ((1, TOKENS), f32, VMEM)]
    steps = HALF // STEP
    scratch = [
        pltpu.VMEM((TOKENS, HALF), bf16),
        pltpu.VMEM((steps, TOKENS, STEP), bf16),
        pltpu.VMEM((TOKENS, TOKENS), f32),
        pltpu.VMEM((TOKENS, TOKENS), bf16),
        pltpu.VMEM((TOKENS, TOKENS), bf16),
        pltpu.VMEM((2 * steps, STEP, TOKENS), bf16),
        pltpu.SemaphoreType.DMA((steps,)),
        pltpu.SemaphoreType.DMA((2 * steps,)),
    ]
    flops = 8 * TOKENS * TOKENS * HALF
    return call(
        last_kernel, outs, ins, scratch, 32, flops, 16 * 2**20, input_output_aliases={1: 0}
    )


def dot(a, b):
    return jnp.dot(a, b, preferred_element_type=f32)


def local(
    head_outputs,
    out_weight,
    residual_input,
    post_gain,
    encoder_weight,
    encoder_bias,
    decoder_weight,
    decoder_bias,
):
    here = lax.axis_index("prod")
    low = here // 2 == 0
    first = here % 2 == 0

    def own_half(v):
        return jnp.where(first, v[..., :HALF], v[..., HALF:])

    def other_half(v):
        return jnp.where(first, v[..., HALF:], v[..., :HALF])

    core = (here % 2).reshape(1)
    partial_value = dot(head_outputs, out_weight)
    both = own_half(partial_value) + to_core(other_half(partial_value))
    encoder_other = cut(encoder_weight, 0, 1 - core, both)
    decoder_other = cut(decoder_weight, 1, 1 - core, both)
    projected = both + lax.ppermute(both, "prod", [(0, 2), (2, 0), (1, 3), (3, 1)])
    projected, encoder_other, decoder_other = lax.optimization_barrier(
        (projected, encoder_other, decoder_other)
    )
    squares = jnp.broadcast_to(jnp.sum(projected * projected, axis=1, keepdims=True), (16, 128))
    squares = (squares + to_core(squares))[:, :1]
    gain = own_half(post_gain)
    normed = projected * lax.rsqrt(squares / D + norm_epsilon) * gain
    stream = (own_half(residual_input).astype(f32) + normed).astype(bf16)
    stream = jnp.where(low, stream, jnp.roll(stream, 8, axis=0))

    stream, encoder_other, decoder_other = lax.optimization_barrier(
        (stream, encoder_other, decoder_other)
    )
    encoder_mate = to_core(encoder_other)
    decoder_mate = to_core(decoder_other)
    bias_own = own_half(decoder_bias)
    stream = jnp.concatenate([stream, to_y(stream, 3)])
    stream = jnp.concatenate([stream] + [to_minor(stream, -d) for d in (1, 2, 3)])
    own_stream = stream.reshape(4, 4, 8, HALF)[:, 0].reshape(32, HALF)
    centred = (stream.astype(f32) - bias_own).astype(bf16)
    centred, encoder_mate, decoder_mate = lax.optimization_barrier(
        (centred, encoder_mate, decoder_mate)
    )
    encoder_mate = cut(encoder_mate, 0, core * 0, centred)
    decoder_mate = cut(decoder_mate, 1, core * 0, centred)
    encoder_own = cut(encoder_weight, 0, core, centred)
    decoder_own = cut(decoder_weight, 1, core, centred)
    centred = [centred] + [to_major(centred, -d) for d in (1, 2, 3)]

    for_mate = swap_blocks(jnp.concatenate([dot(piece, encoder_mate) for piece in centred]))
    decoder_other, norms, penalty = decoder_rows(core, centred[0], decoder_weight, decoder_own)
    for_mate, decoder_own, decoder_mate, decoder_other, norms, penalty = lax.optimization_barrier(
        (for_mate, decoder_own, decoder_mate, decoder_other, norms, penalty)
    )
    preact = jnp.concatenate([dot(piece, encoder_own) for piece in centred])
    preact = preact + to_core(for_mate.astype(bf16)).astype(f32) + encoder_bias
    rectified = jnp.maximum(preact, 0.0)
    activations = jnp.square(rectified).astype(bf16)
    swapped = swap_blocks(activations)
    mate_activations = to_core(swapped)

    own = product(activations, decoder_own)
    pieces = {}
    for d in range(4):
        rows = slice(128 * d, 128 * d + 128)
        pieces[d] = (own[rows] + dot(mate_activations[rows], decoder_mate)).astype(bf16)
    far = pieces[2].reshape(4, 4, 8, HALF)
    keep = jnp.where(first, far[:, :2], far[:, ::2])
    send = jnp.where(first, far[:, 2:], far[:, 1::2])
    send = move(send, lambda x, y, z, c: (x, y ^ (3 if c == 0 else 1), z, c))
    far = (keep.astype(f32) + send.astype(f32)).astype(bf16)
    send = move(far[:, 1], lambda x, y, z, c: (x, y ^ (1 if c == 0 else 3), z, c))
    far = (far[:, 0].astype(f32) + send.astype(f32)).astype(bf16).reshape(32, HALF)
    recon = [pieces[0], to_major(pieces[1], 1), to_major(pieces[3], 3)]
    recon = sum(piece.astype(f32) for piece in recon).astype(bf16)
    flipped_own, flipped_act, flipped_swapped, factor = flip(
        centred, [activations, swapped], norms, pieces[0]
    )
    recon, flipped_own = lax.optimization_barrier((recon, flipped_own))
    flipped_mate = to_core(flipped_own)
    recon = (scatter_y(recon) + to_major(far, 2).astype(f32)).astype(bf16)
    summed = recon.astype(f32)
    for d in (1, 2, 3):
        summed = summed + jnp.roll(to_minor(recon, -d), 8 * d, axis=0).astype(f32)
    grad_recon = (2.0 * (summed + bias_own - own_stream.astype(f32)) / TOKENS).astype(bf16)

    far = to_major(grad_recon, 2)
    errors = gather_y(grad_recon)
    errors, flipped_mate = lax.optimization_barrier((errors, flipped_mate))
    errors = [errors, to_major(errors, -1), gather_y(far), to_major(errors, -3)]
    errors_mate = [to_core(piece) for piece in errors]

    grad_acts, grad_decoder = first_gradients(core, errors, decoder_own, flipped_act, factor)
    grad_decoder, grad_encoder, grad_bias = last_gradients(
        core, grad_decoder, grad_acts, errors_mate, decoder_other, flipped_swapped, factor,
        penalty, rectified, flipped_own, flipped_mate,
    )
    return (grad_encoder, grad_bias.reshape(TOKENS), grad_decoder)


def solution(mesh):
    placed = (
        P("sae", "prod"),
        P("prod", None),
        P("sae", None),
        P(),
        P(None, ("prod", "sae")),
        P(("prod", "sae")),
        P(("prod", "sae"), None),
        P(),
    )
    return jax.shard_map(
        local,
        mesh=mesh,
        in_specs=placed,
        out_specs=(P(None, ("prod", "sae")), P(("prod", "sae")), P(("prod", "sae"), None)),
        check_vma=False,
    )
```
